128 devices in a mesh: src: 16 (over x, y), tgt: 8 (over z, core).
Axes of the slice: x: 4, y: 4, z: 4, core: 2. Of those that a mesh axis runs over, the one named last changes fastest.
Arguments:
- source_emb: bfloat16 [64, 1024, 768], P('src', 'tgt')
- target_emb: bfloat16 [32, 1024, 768], P('tgt', 'src')
- slot_source: int32 [16, 8, 6], P('src', 'tgt'), may hold values from 0 to 63, as said below
- slot_target: int32 [16, 8, 6], P('src', 'tgt'), may hold values from 0 to 31, as said below
Outputs:
- log_posterior: float32 [16, 8, 6, 1024, 1024], P('src', 'tgt')
- row_potential: float32 [64, 1024], P('src')
- column_potential: float32 [32, 1024], P('tgt')
The draws below stay inside these ranges and needn't reach their ends.
Inputs may be any that keep to these rules, and one draw needn't show every extreme that they name: `slot_source`: the slots of the worker at index t of tgt name target blocks of that index, t * 4 to (t + 1) * 4 - 1. The 6 slots of one worker name source blocks of distinct indices of src (block // 4). No pair of blocks is named twice, and every source block is named by some slot. `slot_target`: every target block is named by some slot of its index of tgt.
All inputs are finite; a program needn't handle non-finite values.
Results may differ from the reference program's by a relative error of at most 0.0003.
Values may be sent and summed in bfloat16 or wider, within the bound.
No kernel may reach another device: no remote copies, remote signals or barrier semaphores. Data moves between devices by JAX's collectives and lax.ppermute only.
A program may use at most 192 MiB of HBM per device.

```python
import math
import jax
import jax.numpy as jnp
from jax import lax

D = 768
BLOCK = 1024
SBD = 4
TBD = 4
TILE_DEV = 6
ITERS = 3
NSB = 64
NTB = 32
N_SRC = 16
N_TGT = 8


def plan_tiles(key):
    top = min(3 * TILE_DEV, N_SRC, SBD * TBD)
    rest_total = N_TGT * TILE_DEV - top
    pattern = [top] + [j * rest_total // (N_TGT - 1) - (j - 1) * rest_total // (N_TGT - 1) for j in range(1, N_TGT)]
    pattern = jnp.array(pattern, jnp.int32)
    key_rot, key_src, key_tgt = jax.random.split(key, 3)
    groups_count = N_SRC // N_TGT
    rotation = jax.vmap(lambda sub: jax.random.permutation(sub, N_TGT))(jax.random.split(key_rot, groups_count)).reshape(N_SRC)
    columns = jnp.arange(N_TGT)
    counts = pattern[(columns[None, :] + rotation[:, None]) % N_TGT]
    offsets = jnp.cumsum(counts, axis=0) - counts
    src_shift = jax.random.randint(key_src, (N_SRC, N_TGT, 1), 0, SBD)
    tgt_shift = jax.random.randint(key_tgt, (N_SRC, N_TGT, 1), 0, TBD)
    candidate = jnp.arange(SBD * TBD)
    first_part = candidate % SBD
    second_part = (candidate // SBD + candidate % SBD) % TBD
    local_src = (first_part[None, None, :] + src_shift) % SBD
    local_tgt = (second_part[None, None, :] + tgt_shift) % TBD
    position = offsets[:, :, None] + candidate[None, None, :]
    valid = candidate[None, None, :] < counts[:, :, None]
    worker = position % N_SRC
    slot_index = jnp.where(valid, position // N_SRC, TILE_DEV)
    homes = jnp.arange(N_SRC)[:, None, None]
    column_ids = jnp.broadcast_to(columns[None, :, None], position.shape)
    src_global = homes * SBD + local_src
    tgt_global = column_ids * TBD + local_tgt
    empty = jnp.zeros((N_SRC, N_TGT, TILE_DEV), jnp.int32)
    out_src = empty.at[worker, column_ids, slot_index].set(src_global.astype(jnp.int32), mode='drop')
    out_tgt = empty.at[worker, column_ids, slot_index].set(tgt_global.astype(jnp.int32), mode='drop')
    return (out_src, out_tgt)


def draw_slot_source(key, part):
    return plan_tiles(key)[0]


def draw_slot_target(key, part):
    return plan_tiles(key)[1]


def draw_source_emb(key, part):
    key = jax.random.fold_in(key, 11)
    key_val = jax.random.fold_in(key, 0)
    shape = (NSB, BLOCK, D)
    values = jnp.clip(jax.random.normal(key_val, shape, jnp.float32), -6.0, 6.0)
    return values.astype(jnp.bfloat16)


def draw_target_emb(key, part):
    key = jax.random.fold_in(key, 23)
    key_val = jax.random.fold_in(key, 0)
    shape = (NTB, BLOCK, D)
    values = jnp.clip(jax.random.normal(key_val, shape, jnp.float32), -6.0, 6.0)
    return values.astype(jnp.bfloat16)


def setup_inputs(seed: int = 0) -> dict:
    streams_of = jax.random.split(jax.random.key(seed), 5)
    return {
        "source_emb": draw_source_emb(jax.random.fold_in(streams_of[4], 71), 0),
        "target_emb": draw_target_emb(jax.random.fold_in(streams_of[4], 71), 0),
        "slot_source": draw_slot_source(jax.random.fold_in(streams_of[4], 71), 0),
        "slot_target": draw_slot_target(jax.random.fold_in(streams_of[4], 71), 0),
    }


NEG = -1e+30

def combine_blocks(maxima, totals, labels, groups):
    matches = labels[:, None] == jnp.arange(groups)[None, :]
    largest = lax.optimization_barrier(jnp.max(jnp.where(matches[:, :, None], maxima[:, None, :], NEG), axis=0))
    diffs = jnp.where(matches[:, :, None], maxima[:, None, :] - largest[None, :, :], NEG)
    scaled = jnp.where(matches[:, :, None], totals[:, None, :] * jnp.exp(diffs), 0.0)
    return (largest, lax.optimization_barrier(jnp.sum(scaled, axis=0)))

def reference(source_emb, target_emb, slot_source, slot_target):
    src_ids = slot_source.reshape(-1).astype(jnp.int32)
    tgt_ids = slot_target.reshape(-1).astype(jnp.int32)
    score_scale = 2.0 / math.sqrt(D)

    def tile_score(block_pair):
        source_rows = lax.dynamic_index_in_dim(source_emb, block_pair[0], 0, keepdims=False)
        target_part = lax.dynamic_index_in_dim(target_emb, block_pair[1], 0, keepdims=False)
        return jnp.dot(source_rows, target_part.T, preferred_element_type=jnp.float32) * score_scale
    scores = lax.map(tile_score, jnp.stack([src_ids, tgt_ids], axis=1))
    column_pot = jnp.zeros((NTB, BLOCK), jnp.float32)
    row_pot = jnp.zeros((NSB, BLOCK), jnp.float32)
    for iteration in range(ITERS):

        def row_stats(items):
            shifted = items[0] + column_pot[items[1]][None, :]
            row_max = lax.optimization_barrier(jnp.max(shifted, axis=1))
            return (row_max, lax.optimization_barrier(jnp.sum(jnp.exp(shifted - row_max[:, None]), axis=1)))
        row_max, row_sum = lax.map(row_stats, (scores, tgt_ids))
        largest, summed = combine_blocks(row_max, row_sum, src_ids, NSB)
        row_pot = -(largest + jnp.log(summed))

        def col_stats(items):
            shifted = items[0] + row_pot[items[1]][:, None]
            col_max = lax.optimization_barrier(jnp.max(shifted, axis=0))
            return (col_max, lax.optimization_barrier(jnp.sum(jnp.exp(shifted - col_max[None, :]), axis=0)))
        col_max, col_sum = lax.map(col_stats, (scores, src_ids))
        largest, summed = combine_blocks(col_max, col_sum, tgt_ids, NTB)
        column_pot = -(largest + jnp.log(summed))

    def posterior(items):
        return items[0] + row_pot[items[1]][:, None] + column_pot[items[2]][None, :]
    log_post = lax.map(posterior, (scores, src_ids, tgt_ids))
    return (log_post.reshape(N_SRC, N_TGT, TILE_DEV, BLOCK, BLOCK), row_pot, column_pot)
```

```python
import functools
import math

import jax
import jax.numpy as jnp
from jax import lax
from jax.experimental import pallas as pl
from jax.experimental.pallas import tpu as pltpu
from jax.sharding import PartitionSpec as P

ITERS = 3
NEG = -1e30
F32, BF16 = jnp.float32, jnp.bfloat16
LIMIT = 20.0
ROWS = 512
NT = (((1,), (1,)), ((), ()))


def combine_blocks(maxima, totals, labels, groups):
    matches = labels[:, None] == jnp.arange(groups)[None, :]
    largest = jnp.max(jnp.where(matches[:, :, None], maxima[:, None, :], NEG), axis=0)
    diffs = jnp.where(matches[:, :, None], maxima[:, None, :] - largest[None, :, :], NEG)
    scaled = jnp.where(matches[:, :, None], totals[:, None, :] * jnp.exp(diffs), 0.0)
    return (largest, jnp.sum(scaled, axis=0))


def home_plan(slot_ids, own_row, per_row):
    matched = slot_ids // per_row == own_row
    chosen = jnp.sum(jnp.where(matched, slot_ids % per_row, 0), axis=1)
    return jnp.where(jnp.any(matched, axis=1), chosen, -1)


def select_rows(table, plan):
    picked = jnp.take(table, jnp.maximum(plan, 0), axis=0)
    present = (plan >= 0).reshape((-1,) + (1,) * (table.ndim - 1))
    return jnp.where(present, picked, jnp.zeros((), table.dtype))


def log_domain(pieces, targets, tile_home, tile_tgt, plan_column, src_blocks):
    tgt_blocks, block_rows, features = targets.shape
    src_count = lax.axis_size("src")
    tile_sources = pieces.transpose(1, 0, 2, 3).reshape(pieces.shape[1], block_rows, features)
    tile_targets = jnp.take(targets, tile_tgt, axis=0)
    scores = jnp.einsum("jid,jkd->jik", tile_sources, tile_targets, preferred_element_type=F32) * (
        2.0 / math.sqrt(features)
    )
    column_pot = jnp.zeros((tgt_blocks, block_rows), F32)

    def iterate(_, carry):
        column_pot, _, _ = carry
        tile_col = jnp.take(column_pot, tile_tgt, axis=0)
        shifted = scores + tile_col[:, None, :]
        row_max = jnp.max(shifted, axis=2)
        row_sum = jnp.sum(jnp.exp(shifted - row_max[:, :, None]), axis=2)
        send_max, send_sum = combine_blocks(row_max, row_sum, tile_home, src_count)
        got_max, got_sum = (
            lax.all_to_all(send_max, "src", split_axis=0, concat_axis=0, tiled=True),
            lax.all_to_all(send_sum, "src", split_axis=0, concat_axis=0, tiled=True),
        )
        local_max, local_sum = combine_blocks(got_max, got_sum, plan_column, src_blocks)
        largest = lax.pmax(local_max, "tgt")
        summed = lax.psum(local_sum * jnp.exp(local_max - largest), "tgt")
        row_pot = -(largest + jnp.log(summed))
        returned = lax.all_to_all(
            select_rows(row_pot, plan_column), "src", split_axis=0, concat_axis=0, tiled=True
        )
        tile_row = jnp.take(returned, tile_home, axis=0)
        shifted = scores + tile_row[:, :, None]
        col_max = jnp.max(shifted, axis=1)
        col_sum = jnp.sum(jnp.exp(shifted - col_max[:, None, :]), axis=1)
        local_max, local_sum = combine_blocks(col_max, col_sum, tile_tgt, tgt_blocks)
        largest = lax.pmax(local_max, "src")
        summed = lax.psum(local_sum * jnp.exp(local_max - largest), "src")
        return (-(largest + jnp.log(summed)), row_pot, tile_row)

    init = (column_pot, jnp.zeros((src_blocks, block_rows), F32), jnp.zeros((scores.shape[0], block_rows), F32))
    column_pot, row_pot, tile_row = lax.fori_loop(0, ITERS, iterate, init)
    tile_col = jnp.take(column_pot, tile_tgt, axis=0)
    log_post = scores + tile_row[:, :, None] + tile_col[:, None, :]
    return (log_post[None, None], row_pot, column_pot)


def stack3(x):
    hi = x.astype(BF16).astype(F32)
    mid = (x - hi).astype(BF16).astype(F32)
    low = x - hi - mid
    row = lax.broadcasted_iota(jnp.int32, (16, x.shape[1]), 0)
    parts = [jnp.broadcast_to(p, row.shape) for p in (hi, mid, low)]
    return jnp.where(row == 0, parts[0], jnp.where(row == 1, parts[1], jnp.where(row == 2, parts[2], 0.0))).astype(BF16)


def lane_totals(lanes):
    ones = jnp.ones((8, 128), F32)
    return lax.dot_general(ones, lanes, NT, preferred_element_type=F32, precision=lax.Precision.HIGHEST)[0:1]


def scores_kernel(scale, named, x_ref, y_ref, k_ref, sum_ref, work, lane_sum, lowest):
    blocks, width, _ = y_ref.shape
    per = width // ROWS
    count = blocks * per * blocks

    def product(n, slot):
        work[slot] = lax.dot_general(
            x_ref[n // blocks], y_ref[lax.rem(n, blocks)], NT, preferred_element_type=F32
        )

    def weigh(n, slot):
        i, c = n // blocks, lax.rem(n, blocks)
        e = jnp.exp2(work[slot] * scale)
        k = e.astype(BF16)
        rows = pl.ds(pl.multiple_of(i * ROWS, ROWS), ROWS)
        k_ref[rows, pl.ds(pl.multiple_of(c * width, width), width)] = k
        acc, low = e[:, :128], k[:, :128]
        for g in range(1, width // 128):
            acc = acc + e[:, g * 128 : (g + 1) * 128]
            low = jnp.minimum(low, k[:, g * 128 : (g + 1) * 128])
        here = jnp.where(named[i // per, c] > 0, acc, 0.0)
        lane_sum[i] = jnp.where(c == 0, here, lane_sum[i] + here)
        lowest[...] = jnp.minimum(lowest[...], jnp.min(low.reshape(ROWS // 16, 16, 128), axis=0))

    lowest[...] = jnp.ones_like(lowest)
    lane_sum[...] = jnp.zeros_like(lane_sum)
    product(0, 0)

    def step(m, carry):
        product(m * 2 + 1, 1)
        weigh(m * 2, 0)
        product(jnp.minimum(m * 2 + 2, count - 1), 0)
        weigh(m * 2 + 1, 1)
        return carry

    lax.fori_loop(0, count // 2, step, 0)
    low = jnp.min(lowest[...].astype(F32))
    totals = [lane_totals(lane_sum[i]) for i in range(blocks * per)]
    high = functools.reduce(jnp.maximum, [jnp.max(t) for t in totals])
    fine = (low > math.exp(-LIMIT)) & (high < math.exp(LIMIT))
    for i, total in enumerate(totals):
        total = jnp.where(fine, total, jnp.nan)
        cols = slice((i % per) * ROWS, (i % per + 1) * ROWS)
        sum_ref[:, i // per, :, cols] = jnp.broadcast_to(total[None], (sum_ref.shape[0], 1, ROWS))


def score_weights(x, y, named, copies):
    blocks, width, depth = y.shape
    n = blocks * width
    whole = pl.BlockSpec(memory_space=pltpu.VMEM)
    return pl.pallas_call(
        functools.partial(scores_kernel, 2.0 / math.sqrt(depth) * math.log2(math.e)),
        in_specs=[pl.BlockSpec(memory_space=pltpu.SMEM), whole, whole],
        out_specs=[whole, whole],
        scratch_shapes=[
            pltpu.VMEM((2, ROWS, width), F32),
            pltpu.VMEM((n // ROWS, ROWS, 128), F32),
            pltpu.VMEM((16, 128), BF16),
        ],
        out_shape=[pltpu.VMEM((n, n), BF16), jax.ShapeDtypeStruct((copies, blocks, 1, width), F32)],
        compiler_params=pltpu.CompilerParams(vmem_limit_bytes=26 << 20),
        name="score_weights",
    )(named, x.reshape(n // ROWS, ROWS, depth), y)


def put(o_ref, block, start, out):
    o_ref[:, block, :, start : start + out.shape[1]] = jnp.broadcast_to(out[None], (o_ref.shape[0],) + out.shape)


def column_kernel(named, g_ref, k_in, o_ref, k_ref):
    total = jnp.sum(g_ref[...], axis=0)
    blocks, _, width = total.shape
    fine = (jnp.min(total) > 0.0) & (jnp.max(total) < 1e38)
    spoil = jnp.where(fine, 0.0, jnp.nan)
    lhs = [stack3(1.0 / total[b]) for b in range(blocks)]
    for c in range(blocks):
        live = [jnp.where(named[b, c] > 0, lhs[b], jnp.zeros_like(lhs[b])) for b in range(blocks)]
        for start in range(0, width, ROWS):
            cols = slice(c * width + start, c * width + start + ROWS)
            acc = jnp.zeros((16, ROWS), F32)
            for b in range(blocks):
                acc = acc + jnp.dot(live[b], k_ref[b * width : (b + 1) * width, cols], preferred_element_type=F32)
            put(o_ref, c, start, acc[0:1] + acc[1:2] + acc[2:3] + spoil)


def row_kernel(named, g_ref, k_in, o_ref, k_ref):
    total = jnp.sum(g_ref[...], axis=0)
    blocks, _, width = total.shape
    fine = (jnp.min(total) >= math.exp(-LIMIT)) & (jnp.max(total) <= math.exp(LIMIT))
    spoil = jnp.where(fine, 0.0, jnp.nan)
    inv = 1.0 / total
    half = blocks // 2
    lhs = [stack3(inv[c]) for c in range(half)]
    for b in range(blocks):
        live = [jnp.where(named[b, c] > 0, lhs[c], jnp.zeros_like(lhs[c])) for c in range(half)]
        flat = [jnp.where(named[b, c] > 0, inv[c], jnp.zeros_like(inv[c])) for c in range(half, blocks)]
        for start in range(0, width, ROWS):
            rows = slice(b * width + start, b * width + start + ROWS)
            acc = jnp.zeros((16, ROWS), F32)
            for c in range(half):
                acc = acc + lax.dot_general(
                    live[c], k_ref[rows, c * width : (c + 1) * width], NT, preferred_element_type=F32
                )
            lanes = jnp.zeros((ROWS, 128), F32)
            for c in range(half, blocks):
                for g in range(0, width, 128):
                    part = k_ref[rows, c * width + g : c * width + g + 128].astype(F32)
                    lanes = lanes + part * flat[c - half][:, g : g + 128]
            put(o_ref, b, start, acc[0:1] + acc[1:2] + acc[2:3] + lane_totals(lanes) + spoil)


def weighted_sums(kernel, name, named, gathered, k, copies):
    whole = pl.BlockSpec(memory_space=pltpu.VMEM)
    return pl.pallas_call(
        kernel,
        in_specs=[pl.BlockSpec(memory_space=pltpu.SMEM), whole, whole],
        out_specs=[whole, whole],
        out_shape=[jax.ShapeDtypeStruct((copies,) + gathered.shape[1:], F32), pltpu.VMEM(k.shape, k.dtype)],
        input_output_aliases={2: 1},
        compiler_params=pltpu.CompilerParams(vmem_limit_bytes=12 << 20),
        name=name,
    )(named, gathered, pltpu.with_memory_space_constraint(k, pltpu.VMEM))


def posterior_kernel(scale, tile_tgt, x_ref, y_ref, r_ref, c_ref, o_ref):
    width, depth = y_ref.shape[1:]
    row = jnp.broadcast_to(r_ref[0], (128, width)).T
    x = x_ref[...].reshape(width, depth)
    for start in range(0, width, 256):
        cols = slice(start, start + 256)
        s = lax.dot_general(x, y_ref[0, cols], NT, preferred_element_type=F32) * scale
        for g in range(0, 256, 128):
            out = s[:, g : g + 128] + row + c_ref[0, :, start + g : start + g + 128]
            o_ref[0, 0, 0, :, start + g : start + g + 128] = out


def posterior(pieces, targets, tile_row, column_pot, tile_tgt):
    parts, tiles, piece, depth = pieces.shape
    width = targets.shape[1]
    return pl.pallas_call(
        functools.partial(posterior_kernel, 2.0 / math.sqrt(depth)),
        grid_spec=pltpu.PrefetchScalarGridSpec(
            num_scalar_prefetch=1,
            grid=(tiles,),
            in_specs=[
                pl.BlockSpec((parts, 1, piece, depth), lambda j, t: (0, j, 0, 0)),
                pl.BlockSpec((1, width, depth), lambda j, t: (t[j], 0, 0)),
                pl.BlockSpec((1, 1, width), lambda j, t: (j, 0, 0)),
                pl.BlockSpec((1, 1, width), lambda j, t: (t[j], 0, 0)),
            ],
            out_specs=pl.BlockSpec((1, 1, 1, width, width), lambda j, t: (0, 0, j, 0, 0)),
        ),
        out_shape=jax.ShapeDtypeStruct((1, 1, tiles, width, width), F32),
        compiler_params=pltpu.CompilerParams(vmem_limit_bytes=40 << 20),
        name="posterior",
    )(tile_tgt, pieces, targets, tile_row, column_pot)


def swap(x, axis):
    return lax.all_to_all(x, axis, split_axis=0, concat_axis=0, tiled=True)


def on_device(source_emb, target_emb, slot_source, slot_target):
    src_blocks, tgt_blocks = source_emb.shape[0], target_emb.shape[0]
    src_count, tgt_count = lax.axis_size("src"), lax.axis_size("tgt")
    own_row, own_col = lax.axis_index("src"), lax.axis_index("tgt")
    tiles = slot_source.shape[2]
    tile_src = slot_source[0, 0]
    tile_tgt = slot_target[0, 0] - own_col * tgt_blocks
    tile_home = tile_src // src_blocks

    slots = jnp.concatenate([slot_source[0, 0], slot_target[0, 0]])
    slots = jnp.pad(slots, (0, 128 - 2 * tiles))[None, None]
    column_slots = swap(jnp.broadcast_to(slots, (src_count, 1, 128)), "src")[:, 0]
    row_slots = swap(jnp.broadcast_to(slots, (tgt_count, 1, 128)), "tgt")[:, 0, :tiles]
    named_src = column_slots[:, :tiles].reshape(-1) - own_row * src_blocks
    named_tgt = column_slots[:, tiles : 2 * tiles].reshape(-1) - own_col * tgt_blocks
    named = jnp.any(
        (named_src[:, None, None] == jnp.arange(src_blocks)[None, :, None])
        & (named_tgt[:, None, None] == jnp.arange(tgt_blocks)[None, None, :]),
        axis=0,
    ).astype(jnp.int32)
    plan_column = home_plan(column_slots[:, :tiles], own_row, src_blocks)

    targets = lax.all_gather(target_emb, "src", axis=1, tiled=True)
    whole_blocks = lax.all_gather(source_emb, "tgt", axis=1, tiled=True)
    all_pieces = lax.all_gather(source_emb, "src", axis=0, tiled=True)
    pieces = swap(jnp.take(all_pieces, row_slots, axis=0), "tgt")

    weights, sums = score_weights(whole_blocks, targets, named, tgt_count)
    for iteration in range(ITERS):
        if iteration:
            sums, weights = weighted_sums(row_kernel, "row_sums", named, gathered, weights, tgt_count)
        row_gathered = swap(sums, "tgt")
        sums, weights = weighted_sums(column_kernel, "column_sums", named, row_gathered, weights, src_count)
        gathered = swap(sums, "src")

    row_total = jnp.sum(row_gathered, axis=0)[:, 0]
    row_pot = -jnp.log(row_total)
    column_pot = -jnp.log(jnp.sum(gathered, axis=0))
    tile_row = jnp.take(swap(select_rows(row_pot, plan_column)[:, None], "src"), tile_home, axis=0)
    log_post = posterior(pieces, targets, tile_row, column_pot, tile_tgt)

    def unfinished(carry):
        return carry[0]

    def redo(carry):
        return (jnp.zeros((), jnp.bool_),) + log_domain(
            pieces, targets, tile_home, tile_tgt, plan_column, src_blocks
        )

    out_of_range = jnp.logical_not(row_total[0, 0] > 0.0)
    carry = (out_of_range, log_post, row_pot, column_pot[:, 0])
    return lax.while_loop(unfinished, redo, carry)[1:]


def solution(mesh):
    placed = (
        P("src", "tgt", None),
        P("tgt", "src", None),
        P("src", "tgt", None),
        P("src", "tgt", None),
    )
    return jax.shard_map(
        on_device,
        mesh=mesh,
        in_specs=placed,
        out_specs=(P("src", "tgt", None, None, None), P("src", None), P("tgt", None)),
        check_vma=False,
    )
```

```python
import functools
import math

import jax
import jax.numpy as jnp
from jax import lax
from jax.experimental import pallas as pl
from jax.experimental.pallas import tpu as pltpu
from jax.sharding import PartitionSpec as P

ITERS = 3
NEG = -1e30
F32, BF16 = jnp.float32, jnp.bfloat16
LIMIT = 20.0
ROWS = 512
PARTS = 2
LIGHT = pl.CostEstimate(flops=0, bytes_accessed=1024, transcendentals=0)
NT = (((1,), (1,)), ((), ()))


def combine_blocks(maxima, totals, labels, groups):
    matches = labels[:, None] == jnp.arange(groups)[None, :]
    largest = jnp.max(jnp.where(matches[:, :, None], maxima[:, None, :], NEG), axis=0)
    diffs = jnp.where(matches[:, :, None], maxima[:, None, :] - largest[None, :, :], NEG)
    scaled = jnp.where(matches[:, :, None], totals[:, None, :] * jnp.exp(diffs), 0.0)
    return (largest, jnp.sum(scaled, axis=0))


def home_plan(slot_ids, own_row, per_row):
    matched = slot_ids // per_row == own_row
    chosen = jnp.sum(jnp.where(matched, slot_ids % per_row, 0), axis=1)
    return jnp.where(jnp.any(matched, axis=1), chosen, -1)


def select_rows(table, plan):
    picked = jnp.take(table, jnp.maximum(plan, 0), axis=0, mode="clip")
    present = (plan >= 0).reshape((-1,) + (1,) * (table.ndim - 1))
    return jnp.where(present, picked, jnp.zeros((), table.dtype))


def log_domain(scores, tile_home, tile_tgt, plan_column, src_blocks, tgt_blocks):
    block_rows = scores.shape[1]
    src_count = lax.axis_size("src")

    def iterate(_, carry):
        column_pot, _, _ = carry
        tile_col = jnp.take(column_pot, tile_tgt, axis=0)
        shifted = scores + tile_col[:, None, :]
        row_max = jnp.max(shifted, axis=2)
        row_sum = jnp.sum(jnp.exp(shifted - row_max[:, :, None]), axis=2)
        send_max, send_sum = combine_blocks(row_max, row_sum, tile_home, src_count)
        local_max, local_sum = combine_blocks(swap(send_max, "src"), swap(send_sum, "src"), plan_column, src_blocks)
        largest = lax.pmax(local_max, "tgt")
        summed = lax.psum(local_sum * jnp.exp(local_max - largest), "tgt")
        row_pot = -(largest + jnp.log(summed))
        tile_row = jnp.take(swap(select_rows(row_pot, plan_column), "src"), tile_home, axis=0)
        shifted = scores + tile_row[:, :, None]
        col_max = jnp.max(shifted, axis=1)
        col_sum = jnp.sum(jnp.exp(shifted - col_max[:, None, :]), axis=1)
        local_max, local_sum = combine_blocks(col_max, col_sum, tile_tgt, tgt_blocks)
        largest = lax.pmax(local_max, "src")
        summed = lax.psum(local_sum * jnp.exp(local_max - largest), "src")
        return (-(largest + jnp.log(summed)), row_pot, tile_row)

    init = (
        jnp.zeros((tgt_blocks, block_rows), F32),
        jnp.zeros((src_blocks, block_rows), F32),
        jnp.zeros((scores.shape[0], block_rows), F32),
    )
    return lax.fori_loop(0, ITERS, iterate, init)


def stack3(x):
    hi = x.astype(BF16).astype(F32)
    mid = (x - hi).astype(BF16).astype(F32)
    low = x - hi - mid
    row = lax.broadcasted_iota(jnp.int32, (16, x.shape[1]), 0)
    parts = [jnp.broadcast_to(p, row.shape) for p in (hi, mid, low)]
    return jnp.where(row == 0, parts[0], jnp.where(row == 1, parts[1], jnp.where(row == 2, parts[2], 0.0))).astype(BF16)


def lane_totals(lanes):
    ones = jnp.ones((8, 128), F32)
    return lax.dot_general(ones, lanes, NT, preferred_element_type=F32, precision=lax.Precision.HIGHEST)[0:1]


def put(o_ref, block, cols, out):
    o_ref[:, block, :, cols] = jnp.broadcast_to(out[None], (o_ref.shape[0],) + out.shape)


def start_all(copies):
    for copy in copies:
        copy.start()


def wait_all(copies):
    for copy in copies:
        copy.wait()


def scores_kernel(scale, side, named, where, x_hbm, *refs):
    pieces, refs = refs[:8], refs[-11:]
    k_hbm, sum_ref, targets_hbm, x, y, k_out, lowest, x_sem, y_sem, k_sem, leave = refs
    blocks, width, _ = y.shape
    rows = k_out.shape[1]
    half = blocks // 2
    small = width // (side * side)

    def target_copy(route, far, near):
        first = lax.rem(where[route] - near + side, side)
        second = lax.rem(where[1 - route] - far + side, side)
        at = (first * side + second if route == 0 else second * side + first) * small
        return pltpu.make_async_copy(
            pieces[route * side + far].at[near],
            y.at[pl.ds(route * half, half), pl.ds(pl.multiple_of(at, small), small), :],
            y_sem.at[route, far, near],
        )

    def target_copies(route):
        return [target_copy(route, far, near) for far in range(side) for near in range(side)]

    def source_copy(b):
        return pltpu.make_async_copy(x_hbm.at[b], x.at[b], x_sem.at[b])

    def out_copy(i, slot):
        at = pl.ds(pl.multiple_of(i * rows, rows), rows)
        return pltpu.make_async_copy(k_out.at[slot], k_hbm.at[at], k_sem.at[slot])

    start_all(target_copies(0))
    source_copy(0).start()
    start_all(target_copies(1))
    start_all([source_copy(b) for b in range(1, blocks)])
    lowest[...] = jnp.ones_like(lowest)
    wait_all(target_copies(0) + target_copies(1))
    whole_targets = pltpu.make_async_copy(y, targets_hbm, leave)
    whole_targets.start()
    per = width // rows

    def step(i, carry):
        b, part, slot = i // per, lax.rem(i, per), lax.rem(i, 2)

        @pl.when(part == 0)
        def _():
            source_copy(b).wait()

        @pl.when(i >= 2)
        def _():
            out_copy(i - 2, slot).wait()

        low = lowest[...]
        lanes = jnp.zeros((rows, 128), F32)
        here = x[b, pl.ds(pl.multiple_of(part * rows, rows), rows), :]
        for c in range(blocks):
            s = lax.dot_general(here, y[c], NT, preferred_element_type=F32)
            e = jnp.exp2(s * scale)
            k = e.astype(BF16)
            is_named = named[b, c] > 0
            k_out[slot, :, c * width : (c + 1) * width] = jnp.where(is_named, k, jnp.zeros_like(k))
            acc, least = e[:, :128], k[:, :128]
            for g in range(128, width, 128):
                acc = acc + e[:, g : g + 128]
                least = jnp.minimum(least, k[:, g : g + 128])
            lanes = lanes + jnp.where(is_named, acc, 0.0)
            low = jnp.minimum(low, jnp.min(least.reshape(rows // 16, 16, 128), axis=0))
        lowest[...] = low
        out_copy(i, slot).start()
        total = lane_totals(lanes)
        fine = (jnp.min(low.astype(F32)) > math.exp(-LIMIT)) & (jnp.max(total) < math.exp(LIMIT))
        put(sum_ref, b, pl.ds(pl.multiple_of(part * rows, rows), rows), jnp.where(fine, total, jnp.nan))
        return carry

    lax.fori_loop(0, blocks * per, step, 0)
    for i in (blocks * per - 2, blocks * per - 1):
        out_copy(i, i % 2).wait()
    whole_targets.wait()


ANYWHERE = pl.BlockSpec(memory_space=pl.ANY)
SCALARS = pl.BlockSpec(memory_space=pltpu.SMEM)
WHOLE = pl.BlockSpec(memory_space=pltpu.VMEM)


def far(arrays):
    return [pltpu.with_memory_space_constraint(x, pltpu.HBM) for x in arrays]


def score_weights(x, pieces, where, named, copies, side, after):
    blocks, width, depth = x.shape
    n = blocks * width
    return pl.pallas_call(
        functools.partial(scores_kernel, 2.0 / math.sqrt(depth) * math.log2(math.e), side),
        in_specs=[SCALARS, SCALARS] + [ANYWHERE] * (9 + len(after)),
        out_specs=[ANYWHERE, WHOLE, ANYWHERE],
        scratch_shapes=[
            pltpu.VMEM((blocks, width, depth), BF16),
            pltpu.VMEM((blocks, width, depth), BF16),
            pltpu.VMEM((2, ROWS, n), BF16),
            pltpu.VMEM((16, 128), BF16),
            pltpu.SemaphoreType.DMA((blocks,)),
            pltpu.SemaphoreType.DMA((2, side, side)),
            pltpu.SemaphoreType.DMA((2,)),
            pltpu.SemaphoreType.DMA,
        ],
        out_shape=[
            jax.ShapeDtypeStruct((n, n), BF16),
            jax.ShapeDtypeStruct((copies, blocks, 1, width), F32),
            jax.ShapeDtypeStruct((blocks, width, depth), BF16),
        ],
        compiler_params=pltpu.CompilerParams(vmem_limit_bytes=44 << 20),
        cost_estimate=LIGHT,
        name="score_weights",
    )(named, where, *far([x, *pieces, *after]))


def inverse_parts(g_ref, low, high):
    total = jnp.sum(g_ref[...], axis=0)
    fine = (jnp.min(total) >= low) & (jnp.max(total) <= high)
    return [1.0 / total[b] for b in range(total.shape[0])], jnp.where(fine, 0.0, jnp.nan)


def column_kernel(g_ref, k_hbm, *refs):
    o_ref, k, sem = refs[-3:]
    parts, n, cols = k.shape
    copies = [pltpu.make_async_copy(k_hbm.at[:, pl.ds(j * cols, cols)], k.at[j], sem.at[j]) for j in range(parts)]
    start_all(copies)
    inv, spoil = inverse_parts(g_ref, 1e-38, 1e38)
    blocks, width = len(inv), inv[0].shape[1]
    lhs = [stack3(v) for v in inv]
    per = width // cols
    for j in range(parts):
        copies[j].wait()
        acc = jnp.zeros((16, cols), F32)
        for b in range(blocks):
            acc = acc + jnp.dot(lhs[b], k[j, b * width : (b + 1) * width, :], preferred_element_type=F32)
        start = (j % per) * cols
        put(o_ref, j // per, slice(start, start + cols), acc[0:1] + acc[1:2] + acc[2:3] + spoil)


def row_kernel(g_ref, k_hbm, *refs):
    o_ref, k, sem = refs[-3:]
    parts, rows, n = k.shape
    copies = [pltpu.make_async_copy(k_hbm.at[pl.ds(j * rows, rows)], k.at[j], sem.at[j]) for j in range(parts)]
    start_all(copies)
    inv, spoil = inverse_parts(g_ref, math.exp(-LIMIT), math.exp(LIMIT))
    blocks, width = len(inv), inv[0].shape[1]
    half = blocks // 2
    lhs = [stack3(v) for v in inv[:half]]
    per = width // rows
    for j in range(parts):
        copies[j].wait()
        acc = jnp.zeros((16, rows), F32)
        for c in range(half):
            acc = acc + lax.dot_general(
                lhs[c], k[j, :, c * width : (c + 1) * width], NT, preferred_element_type=F32
            )
        lanes = jnp.zeros((rows, 128), F32)
        for c in range(half, blocks):
            for g in range(0, width, 128):
                at = c * width + g
                lanes = lanes + k[j, :, at : at + 128].astype(F32) * inv[c][:, g : g + 128]
        start = (j % per) * rows
        put(o_ref, j // per, slice(start, start + rows), acc[0:1] + acc[1:2] + acc[2:3] + lane_totals(lanes) + spoil)


def weighted_sums(kernel, gathered, k, copies, after=()):
    n = k.shape[0]
    parts = n // ROWS
    shape = (parts, n, ROWS) if kernel is column_kernel else (parts, ROWS, n)
    return pl.pallas_call(
        kernel,
        in_specs=[WHOLE, ANYWHERE] + [ANYWHERE] * len(after),
        out_specs=WHOLE,
        out_shape=jax.ShapeDtypeStruct((copies,) + gathered.shape[1:], F32),
        scratch_shapes=[pltpu.VMEM(shape, BF16), pltpu.SemaphoreType.DMA((parts,))],
        compiler_params=pltpu.CompilerParams(vmem_limit_bytes=44 << 20),
        cost_estimate=LIGHT,
        name="column_sums" if kernel is column_kernel else "row_sums",
    )(gathered, *far([k, *after]))


def cut_kernel(x_ref, *refs):
    outs = refs[-PARTS:]
    rows = outs[0].shape[1]
    for part, out in enumerate(outs):
        out[...] = x_ref[:, part * rows : (part + 1) * rows, :]


def cut(x, after):
    shape = (x.shape[0], x.shape[1] // PARTS, x.shape[2])
    return pl.pallas_call(
        cut_kernel,
        in_specs=[WHOLE] + [ANYWHERE] * len(after),
        out_specs=[WHOLE] * PARTS,
        out_shape=[jax.ShapeDtypeStruct(shape, x.dtype)] * PARTS,
        compiler_params=pltpu.CompilerParams(vmem_limit_bytes=16 << 20),
        cost_estimate=LIGHT,
        name="cut_rows",
    )(x, *far(after))


def gate_kernel(x_ref, *refs):
    refs[-1][...] = x_ref[...]


def gate(x, after):
    return pl.pallas_call(
        gate_kernel,
        in_specs=[WHOLE] + [ANYWHERE] * len(after),
        out_specs=WHOLE,
        out_shape=jax.ShapeDtypeStruct(x.shape, x.dtype),
        cost_estimate=LIGHT,
        name="gate",
    )(x, *far(after))


def pick_kernel(ids, table, first, *refs):
    del first
    outs, buf, come, go = refs[:-3], refs[-3], refs[-2], refs[-1]
    groups, tiles = buf.shape[:2]

    def fetch(i, j):
        return pltpu.make_async_copy(table.at[ids[i, j]], buf.at[i, j], come.at[i, j])

    for i in range(groups):
        start_all([fetch(i, j) for j in range(tiles)])
    stores = [pltpu.make_async_copy(buf.at[i], outs[i], go.at[i]) for i in range(groups)]
    for i in range(groups):
        wait_all([fetch(i, j) for j in range(tiles)])
        stores[i].start()
    wait_all(stores)


def pick(table, ids, after):
    groups, tiles = ids.shape
    shape = (tiles,) + table.shape[1:]
    return pl.pallas_call(
        pick_kernel,
        in_specs=[SCALARS, ANYWHERE, ANYWHERE],
        out_specs=[ANYWHERE] * groups,
        out_shape=[jax.ShapeDtypeStruct(shape, table.dtype)] * groups,
        scratch_shapes=[
            pltpu.VMEM((groups,) + shape, table.dtype),
            pltpu.SemaphoreType.DMA((groups, tiles)),
            pltpu.SemaphoreType.DMA((groups,)),
        ],
        compiler_params=pltpu.CompilerParams(vmem_limit_bytes=16 << 20),
        cost_estimate=LIGHT,
        name="pick_pieces",
    )(ids, *far([table, after]))


def posterior_kernel(scale, count, tile_tgt, places, *refs):
    x_hbm, refs = refs[:count], refs[count:]
    y_hbm, r_ref, c_ref, o_hbm, x, y, o, x_sem, y_sem, o_sem = refs
    tiles, width, depth = x.shape
    piece = x_hbm[0].shape[1]
    groups = count // PARTS
    cuts = o_sem.shape[1]
    rows = width // cuts

    def x_copies(j):
        return [
            pltpu.make_async_copy(
                x_hbm[part * groups + p].at[j],
                x.at[j, pl.ds(pl.multiple_of((places[p] * PARTS + part) * piece, piece), piece)],
                x_sem.at[j, part, p],
            )
            for part in range(PARTS)
            for p in range(groups)
        ]

    def y_copy(j):
        return pltpu.make_async_copy(y_hbm.at[tile_tgt[j]], y.at[j], y_sem.at[j])

    def o_copy(j, q):
        at = pl.ds(q * rows, rows)
        return pltpu.make_async_copy(o.at[j, at], o_hbm.at[0, 0, j, at], o_sem.at[j, q])

    for j in range(tiles):
        y_copy(j).start()
        start_all(x_copies(j))

    def step(j, carry):
        y_copy(j).wait()
        wait_all(x_copies(j))
        col = c_ref[tile_tgt[j]]
        for q in range(cuts):
            at = slice(q * rows, (q + 1) * rows)
            row = jnp.broadcast_to(r_ref[j, :, at], (128, rows)).T
            for start in range(0, width, 256):
                s = lax.dot_general(x[j, at], y[j, start : start + 256], NT, preferred_element_type=F32) * scale
                for g in range(0, 256, 128):
                    cols = slice(start + g, start + g + 128)
                    o[j, at, cols] = s[:, g : g + 128] + row + col[:, cols]
            o_copy(j, q).start()
        return carry

    lax.fori_loop(0, tiles, step, 0)
    for j in range(tiles):
        wait_all([o_copy(j, q) for q in range(cuts)])


def posterior(pieces, places, targets, tile_row, column_pot, tile_tgt):
    tiles, _, depth = pieces[0].shape
    width = targets.shape[1]
    cuts = 2
    return pl.pallas_call(
        functools.partial(posterior_kernel, 2.0 / math.sqrt(depth), len(pieces)),
        in_specs=[SCALARS, SCALARS] + [ANYWHERE] * (len(pieces) + 1) + [WHOLE, WHOLE],
        out_specs=ANYWHERE,
        scratch_shapes=[
            pltpu.VMEM((tiles, width, depth), BF16),
            pltpu.VMEM((tiles, width, depth), BF16),
            pltpu.VMEM((tiles, width, width), F32),
            pltpu.SemaphoreType.DMA((tiles, PARTS, len(pieces) // PARTS)),
            pltpu.SemaphoreType.DMA((tiles,)),
            pltpu.SemaphoreType.DMA((tiles, cuts)),
        ],
        out_shape=jax.ShapeDtypeStruct((1, 1, tiles, width, width), F32),
        compiler_params=pltpu.CompilerParams(vmem_limit_bytes=54 << 20),
        cost_estimate=LIGHT,
        name="posterior",
    )(tile_tgt, places, *far([*pieces, targets]), tile_row[:, None], column_pot[:, None])


def swap(x, axis):
    return lax.all_to_all(x, axis, split_axis=0, concat_axis=0, tiled=True)


def torus_pieces(shard, side):
    half = shard.shape[0] // 2

    def shift(x, axis, by):
        def to(i):
            a, b = divmod(i, side)
            a, b = ((a + by) % side, b) if axis == 0 else (a, (b + by) % side)
            return a * side + b

        return lax.ppermute(x, "src", [(i, to(i)) for i in range(side * side)])

    pieces = []
    lines = []
    for route, part in enumerate((shard[:half], shard[half:])):
        lines.append(jnp.stack([part] + [shift(part, route, k) for k in range(1, side)]))
    back = [shift(line, 1 - route, 1) for route, line in enumerate(lines)]
    ahead = [shift(line, 1 - route, -1) for route, line in enumerate(lines)]
    mid = side // 2
    for route, line in enumerate(lines):
        far = [shift(back[route][:mid], 1 - route, 1), shift(ahead[route][mid:], 1 - route, -1)]
        pieces += [line, back[route], jnp.concatenate(far), ahead[route]]
    return pieces


def on_device(source_emb, target_emb, slot_source, slot_target):
    src_blocks, tgt_blocks = source_emb.shape[0], target_emb.shape[0]
    src_count, tgt_count = lax.axis_size("src"), lax.axis_size("tgt")
    own_row, own_col = lax.axis_index("src"), lax.axis_index("tgt")
    tiles = slot_source.shape[2]
    tile_src = slot_source[0, 0]
    tile_tgt = slot_target[0, 0] - own_col * tgt_blocks
    tile_home = tile_src // src_blocks

    cores = 2
    length = tgt_count // cores
    turns = [(far, other) for far in range(length) for other in range(cores)]

    def turned(t, far, other):
        return (t // cores + far) % length * cores + (t % cores + other) % cores

    def turn(x, far, other):
        return lax.ppermute(x, "tgt", [(t, turned(t, far, other)) for t in range(tgt_count)])

    places = jnp.stack([turned(own_col, length - far, other) for far, other in turns])

    whole_blocks = lax.all_gather(source_emb, "tgt", axis=1, tiled=True)
    side = math.isqrt(src_count)
    target_pieces = torus_pieces(target_emb, side)

    slots = jnp.concatenate([slot_source[0, 0], slot_target[0, 0]])
    slots = jnp.pad(slots, (0, 128 - 2 * tiles))[None, None]
    column_slots = swap(jnp.broadcast_to(slots, (src_count, 1, 128)), "src")[:, 0]
    row_slots = swap(jnp.broadcast_to(slots, (tgt_count, 1, 128)), "tgt")[:, 0, :tiles]
    named_src = column_slots[:, :tiles].reshape(-1) - own_row * src_blocks
    named_tgt = column_slots[:, tiles : 2 * tiles].reshape(-1) - own_col * tgt_blocks
    named = jnp.any(
        (named_src[:, None, None] == jnp.arange(src_blocks)[None, :, None])
        & (named_tgt[:, None, None] == jnp.arange(tgt_blocks)[None, None, :]),
        axis=0,
    ).astype(jnp.int32)
    plan_column = home_plan(column_slots[:, :tiles], own_row, src_blocks)

    aims = row_slots[jnp.stack([turned(own_col, far, other) for far, other in turns])]
    shards = cut(source_emb, [whole_blocks, named] + target_pieces)
    tables = [lax.all_gather(shard, "src", axis=0, tiled=True) for shard in shards]
    where = jnp.stack([own_row // side, own_row % side])
    weights, sums, targets = score_weights(whole_blocks, target_pieces, where, named, tgt_count, side, shards)
    pieces = [[None] * len(turns) for _ in range(PARTS)]
    beside = [0] + [i for i, (far, _) in enumerate(turns) if far % 2]
    across = [i for i in range(len(turns)) if i not in beside]
    stages = [(0, beside), (0, across), (1, list(range(len(turns))))]
    picked = []
    for (part, chosen), iteration in zip(stages, range(ITERS)):
        if iteration:
            sums = weighted_sums(row_kernel, gathered, weights, tgt_count, after=picked)
            sums = gate(sums, arrived)
        row_gathered = swap(sums, "tgt")
        sums = weighted_sums(column_kernel, row_gathered, weights, src_count)
        picked = list(pick(tables[part], aims[jnp.array(chosen)], row_gathered))
        arrived = [turn(x, *turns[i]) if i else x for x, i in zip(picked, chosen)]
        for x, i in zip(arrived, chosen):
            pieces[part][i] = x
        gathered = swap(sums, "src")
    pieces = pieces[0] + pieces[1]

    row_total = jnp.sum(row_gathered, axis=0)[:, 0]
    row_pot = -jnp.log(row_total)
    column_pot = -jnp.log(jnp.sum(gathered, axis=0)[:, 0])
    tile_row = jnp.take(swap(select_rows(row_pot, plan_column), "src"), tile_home, axis=0, mode="clip")

    def unfinished(carry):
        return carry[0]

    def redo(carry):
        zeros = [jnp.zeros_like(carry[1]), jnp.zeros_like(carry[3])]
        scores = posterior(pieces, places, targets, zeros[1], zeros[0], tile_tgt)[0, 0]
        potentials = log_domain(scores, tile_home, tile_tgt, plan_column, src_blocks, tgt_blocks)
        return (jnp.zeros((), jnp.bool_),) + potentials

    out_of_range = jnp.logical_not(row_total[0, 0] > 0.0)
    carry = (out_of_range, column_pot, row_pot, tile_row)
    _, column_pot, row_pot, tile_row = lax.while_loop(unfinished, redo, carry)
    log_post = posterior(pieces, places, targets, tile_row, column_pot, tile_tgt)
    return (log_post, row_pot, column_pot)


def solution(mesh):
    placed = (
        P("src", "tgt", None),
        P("tgt", "src", None),
        P("src", "tgt", None),
        P("src", "tgt", None),
    )
    return jax.shard_map(
        on_device,
        mesh=mesh,
        in_specs=placed,
        out_specs=(P("src", "tgt", None, None, None), P("src", None), P("tgt", None)),
        check_vma=False,
    )
```

```python
import functools
import math

import jax
import jax.numpy as jnp
from jax import lax
from jax.experimental import pallas as pl
from jax.experimental.pallas import tpu as pltpu
from jax.sharding import PartitionSpec as P

ITERS = 3
NEG = -1e30
F32, BF16 = jnp.float32, jnp.bfloat16
LIMIT = 20.0
ROWS = 512
BLOCKS = 4
PARTS = (64, 64)
LIGHT = pl.CostEstimate(flops=0, bytes_accessed=1024, transcendentals=0)
NT = (((1,), (1,)), ((), ()))


def combine_blocks(maxima, totals, labels, groups):
    matches = labels[:, None] == jnp.arange(groups)[None, :]
    largest = jnp.max(jnp.where(matches[:, :, None], maxima[:, None, :], NEG), axis=0)
    diffs = jnp.where(matches[:, :, None], maxima[:, None, :] - largest[None, :, :], NEG)
    scaled = jnp.where(matches[:, :, None], totals[:, None, :] * jnp.exp(diffs), 0.0)
    return (largest, jnp.sum(scaled, axis=0))


def home_plan(slot_ids, own_row, per_row):
    matched = slot_ids // per_row == own_row
    chosen = jnp.sum(jnp.where(matched, slot_ids % per_row, 0), axis=1)
    return jnp.where(jnp.any(matched, axis=1), chosen, -1)


def select_rows(table, plan):
    picked = jnp.take(table, jnp.maximum(plan, 0), axis=0, mode="clip")
    present = (plan >= 0).reshape((-1,) + (1,) * (table.ndim - 1))
    return jnp.where(present, picked, jnp.zeros((), table.dtype))


def log_domain(scores, tile_home, tile_tgt, plan_column, src_blocks, tgt_blocks):
    block_rows = scores.shape[1]
    src_count = lax.axis_size("src")

    def iterate(_, carry):
        column_pot, _, _ = carry
        tile_col = jnp.take(column_pot, tile_tgt, axis=0)
        shifted = scores + tile_col[:, None, :]
        row_max = jnp.max(shifted, axis=2)
        row_sum = jnp.sum(jnp.exp(shifted - row_max[:, :, None]), axis=2)
        send_max, send_sum = combine_blocks(row_max, row_sum, tile_home, src_count)
        local_max, local_sum = combine_blocks(swap(send_max, "src"), swap(send_sum, "src"), plan_column, src_blocks)
        largest = lax.pmax(local_max, "tgt")
        summed = lax.psum(local_sum * jnp.exp(local_max - largest), "tgt")
        row_pot = -(largest + jnp.log(summed))
        tile_row = jnp.take(swap(select_rows(row_pot, plan_column), "src"), tile_home, axis=0)
        shifted = scores + tile_row[:, :, None]
        col_max = jnp.max(shifted, axis=1)
        col_sum = jnp.sum(jnp.exp(shifted - col_max[:, None, :]), axis=1)
        local_max, local_sum = combine_blocks(col_max, col_sum, tile_tgt, tgt_blocks)
        largest = lax.pmax(local_max, "src")
        summed = lax.psum(local_sum * jnp.exp(local_max - largest), "src")
        return (-(largest + jnp.log(summed)), row_pot, tile_row)

    init = (
        jnp.zeros((tgt_blocks, block_rows), F32),
        jnp.zeros((src_blocks, block_rows), F32),
        jnp.zeros((scores.shape[0], block_rows), F32),
    )
    return lax.fori_loop(0, ITERS, iterate, init)


def stack3(x):
    hi = x.astype(BF16).astype(F32)
    mid = (x - hi).astype(BF16).astype(F32)
    low = x - hi - mid
    row = lax.broadcasted_iota(jnp.int32, (16, x.shape[1]), 0)
    parts = [jnp.broadcast_to(p, row.shape) for p in (hi, mid, low)]
    return jnp.where(row == 0, parts[0], jnp.where(row == 1, parts[1], jnp.where(row == 2, parts[2], 0.0))).astype(BF16)


def lane_totals(lanes):
    ones = jnp.ones((8, 128), F32)
    return lax.dot_general(ones, lanes, NT, preferred_element_type=F32, precision=lax.Precision.HIGHEST)[0:1]


def put(o_ref, block, cols, out):
    o_ref[:, block, :, cols] = jnp.broadcast_to(out[None], (o_ref.shape[0],) + out.shape)


def all_within(x, low, high):
    return jnp.min(jnp.where((x >= low) & (x <= high), 1.0, 0.0)) > 0.0


def start_all(copies):
    for copy in copies:
        copy.start()


def wait_all(copies):
    for copy in copies:
        copy.wait()


def scores_kernel(scale, side, named, where, extra, x_hbm, *refs):
    pieces, refs = refs[:10], refs[-11:]
    k_hbm, sum_ref, targets_hbm, x, y, k_out, lowest, x_sem, y_sem, k_sem, leave = refs
    blocks, width, _ = y.shape
    rows = k_out.shape[1]
    half = blocks // 2
    mid = side // 2
    small = width // (side * side)

    def target_copy(route, far, near):
        first = lax.rem(where[route] - near + side, side)
        second = lax.rem(where[1 - route] - far + side, side)
        at = (first * side + second if route == 0 else second * side + first) * small
        stage, entry = far, near
        if far >= mid:
            stage, entry = (far, near) if far == mid and near < mid else (far + 1, near - mid if far == mid else near)
        return pltpu.make_async_copy(
            pieces[route * (side + 1) + stage].at[entry],
            y.at[pl.ds(route * half, half), pl.ds(pl.multiple_of(at, small), small), :],
            y_sem.at[route, far, near],
        )

    def target_copies(route):
        return [target_copy(route, far, near) for far in range(side) for near in range(side)]

    def source_copy(b):
        return pltpu.make_async_copy(x_hbm.at[b], x.at[b], x_sem.at[b])

    def out_copy(i, slot):
        at = pl.ds(pl.multiple_of(i * rows, rows), rows)
        return pltpu.make_async_copy(k_out.at[slot], k_hbm.at[at], k_sem.at[slot])

    start_all(target_copies(0))
    source_copy(0).start()
    start_all(target_copies(1))
    start_all([source_copy(b) for b in range(1, blocks)])
    lowest[...] = jnp.ones_like(lowest)
    put(sum_ref, blocks, slice(None), extra[...])
    wait_all(target_copies(0) + target_copies(1))
    whole_targets = pltpu.make_async_copy(y, targets_hbm, leave)
    whole_targets.start()
    per = width // rows

    def step(i, carry):
        b, part, slot = i // per, lax.rem(i, per), lax.rem(i, 2)

        @pl.when(part == 0)
        def _():
            source_copy(b).wait()

        @pl.when(i >= 2)
        def _():
            out_copy(i - 2, slot).wait()

        low = lowest[...]
        lanes = jnp.zeros((rows, 128), F32)
        here = x[b, pl.ds(pl.multiple_of(part * rows, rows), rows), :]
        for c in range(blocks):
            s = lax.dot_general(here, y[c], NT, preferred_element_type=F32)
            e = jnp.exp2(s * scale)
            k = e.astype(BF16)
            is_named = named[b, c] > 0
            k_out[slot, :, c * width : (c + 1) * width] = jnp.where(is_named, k, jnp.zeros_like(k))
            acc, least = e[:, :128], k[:, :128]
            for g in range(128, width, 128):
                acc = acc + e[:, g : g + 128]
                least = jnp.minimum(least, k[:, g : g + 128])
            lanes = lanes + jnp.where(is_named, acc, 0.0)
            low = jnp.minimum(low, jnp.min(least.reshape(rows // 16, 16, 128), axis=0))
        lowest[...] = low
        out_copy(i, slot).start()
        total = lane_totals(lanes)
        fine = (jnp.min(low.astype(F32)) > math.exp(-LIMIT)) & all_within(total, 0.0, math.exp(LIMIT))
        put(sum_ref, b, pl.ds(pl.multiple_of(part * rows, rows), rows), jnp.where(fine, total, jnp.nan))
        return carry

    lax.fori_loop(0, blocks * per, step, 0)
    for i in (blocks * per - 2, blocks * per - 1):
        out_copy(i, i % 2).wait()
    whole_targets.wait()


ANYWHERE = pl.BlockSpec(memory_space=pl.ANY)
SCALARS = pl.BlockSpec(memory_space=pltpu.SMEM)
WHOLE = pl.BlockSpec(memory_space=pltpu.VMEM)


def far(arrays):
    return [pltpu.with_memory_space_constraint(x, pltpu.HBM) for x in arrays]


def score_weights(x, pieces, where, named, extra, copies, side, after):
    blocks, width, depth = x.shape
    n = blocks * width
    return pl.pallas_call(
        functools.partial(scores_kernel, 2.0 / math.sqrt(depth) * math.log2(math.e), side),
        in_specs=[SCALARS, SCALARS, WHOLE] + [ANYWHERE] * (1 + len(pieces) + len(after)),
        out_specs=[ANYWHERE, WHOLE, ANYWHERE],
        scratch_shapes=[
            pltpu.VMEM((blocks, width, depth), BF16),
            pltpu.VMEM((blocks, width, depth), BF16),
            pltpu.VMEM((2, ROWS, n), BF16),
            pltpu.VMEM((16, 128), BF16),
            pltpu.SemaphoreType.DMA((blocks,)),
            pltpu.SemaphoreType.DMA((2, side, side)),
            pltpu.SemaphoreType.DMA((2,)),
            pltpu.SemaphoreType.DMA,
        ],
        out_shape=[
            jax.ShapeDtypeStruct((n, n), BF16),
            jax.ShapeDtypeStruct((copies, blocks + 1, 1, width), F32),
            jax.ShapeDtypeStruct((blocks, width, depth), BF16),
        ],
        compiler_params=pltpu.CompilerParams(vmem_limit_bytes=44 << 20),
        cost_estimate=LIGHT,
        name="score_weights",
    )(named, where, extra, *far([x, *pieces, *after]))


def inverse_parts(g_ref, low, high):
    total = jnp.sum(g_ref[:, :BLOCKS], axis=0)
    fine = all_within(total, low, high)
    return [1.0 / total[b] for b in range(total.shape[0])], jnp.where(fine, 0.0, jnp.nan)


def column_kernel(g_ref, k_hbm, *refs):
    columns(g_ref, k_hbm, *refs[-3:])


def last_column_kernel(g_ref, k_hbm, plan, *refs):
    o_ref, k, sem, logs = refs[-4:]
    total = jnp.sum(g_ref[:, :BLOCKS], axis=0)
    logs[...] = -jnp.log(total)
    for s in range(o_ref.shape[0]):
        o_ref[s, total.shape[0]] = logs[jnp.maximum(plan[s], 0)]
    columns(g_ref, k_hbm, o_ref, k, sem)


def columns(g_ref, k_hbm, o_ref, k, sem):
    parts, n, cols = k.shape
    copies = [pltpu.make_async_copy(k_hbm.at[:, pl.ds(j * cols, cols)], k.at[j], sem.at[j]) for j in range(parts)]
    start_all(copies)
    inv, spoil = inverse_parts(g_ref, 1e-38, 1e38)
    blocks, width = len(inv), inv[0].shape[1]
    lhs = [stack3(v) for v in inv]
    per = width // cols
    for j in range(parts):
        copies[j].wait()
        acc = jnp.zeros((16, cols), F32)
        for b in range(blocks):
            acc = acc + jnp.dot(lhs[b], k[j, b * width : (b + 1) * width, :], preferred_element_type=F32)
        start = (j % per) * cols
        put(o_ref, j // per, slice(start, start + cols), acc[0:1] + acc[1:2] + acc[2:3] + spoil)


def row_kernel(g_ref, k_hbm, *refs):
    o_ref, k, sem = refs[-3:]
    parts, rows, n = k.shape
    copies = [pltpu.make_async_copy(k_hbm.at[pl.ds(j * rows, rows)], k.at[j], sem.at[j]) for j in range(parts)]
    start_all(copies)
    inv, spoil = inverse_parts(g_ref, math.exp(-LIMIT), math.exp(LIMIT))
    blocks, width = len(inv), inv[0].shape[1]
    half = blocks // 2
    lhs = [stack3(v) for v in inv[:half]]
    per = width // rows
    for j in range(parts):
        copies[j].wait()
        acc = jnp.zeros((16, rows), F32)
        for c in range(half):
            acc = acc + lax.dot_general(
                lhs[c], k[j, :, c * width : (c + 1) * width], NT, preferred_element_type=F32
            )
        lanes = jnp.zeros((rows, 128), F32)
        for c in range(half, blocks):
            for g in range(0, width, 128):
                at = c * width + g
                lanes = lanes + k[j, :, at : at + 128].astype(F32) * inv[c][:, g : g + 128]
        start = (j % per) * rows
        put(o_ref, j // per, slice(start, start + rows), acc[0:1] + acc[1:2] + acc[2:3] + lane_totals(lanes) + spoil)


def weighted_sums(kernel, gathered, k, copies, after=()):
    n = k.shape[0]
    blocks, width = BLOCKS, gathered.shape[3]
    parts = n // ROWS
    last = kernel is last_column_kernel
    shape = (parts, ROWS, n) if kernel is row_kernel else (parts, n, ROWS)
    return pl.pallas_call(
        kernel,
        in_specs=[WHOLE, ANYWHERE] + [SCALARS] * last + [ANYWHERE] * (len(after) - last),
        out_specs=WHOLE,
        out_shape=jax.ShapeDtypeStruct((copies, blocks + last, 1, width), F32),
        scratch_shapes=[pltpu.VMEM(shape, BF16), pltpu.SemaphoreType.DMA((parts,))]
        + ([pltpu.VMEM((blocks, 1, width), F32)] if last else []),
        compiler_params=pltpu.CompilerParams(vmem_limit_bytes=44 << 20),
        cost_estimate=LIGHT,
        name="row_sums" if kernel is row_kernel else "column_sums",
    )(gathered, *far([k]), *after[:last], *far(after[last:]))


def cut_kernel(x_ref, *refs):
    start = 0
    for out in refs[-len(PARTS) :]:
        rows = out.shape[1]
        out[...] = x_ref[:, start : start + rows, :]
        start += rows


def cut(x, after):
    whole = x.shape[1] // sum(PARTS)
    return pl.pallas_call(
        cut_kernel,
        in_specs=[WHOLE] + [ANYWHERE] * len(after),
        out_specs=[WHOLE] * len(PARTS),
        out_shape=[jax.ShapeDtypeStruct((x.shape[0], rows * whole, x.shape[2]), x.dtype) for rows in PARTS],
        compiler_params=pltpu.CompilerParams(vmem_limit_bytes=16 << 20),
        cost_estimate=LIGHT,
        name="cut_rows",
    )(x, *far(after))


def gate_kernel(x_ref, *refs):
    refs[-1][...] = x_ref[...]


def gate(x, after):
    return pl.pallas_call(
        gate_kernel,
        in_specs=[WHOLE] + [ANYWHERE] * len(after),
        out_specs=WHOLE,
        out_shape=jax.ShapeDtypeStruct(x.shape, x.dtype),
        cost_estimate=LIGHT,
        name="gate",
    )(x, *far(after))


def potentials_kernel(homes, row_ref, col_ref, row_pot, column_pot, tile_row):
    rows = jnp.sum(row_ref[:, :BLOCKS], axis=0)
    columns = jnp.sum(col_ref[:, :BLOCKS], axis=0)
    for b in range(BLOCKS):
        row_pot[b : b + 1] = -jnp.log(rows[b])
        column_pot[b : b + 1] = -jnp.log(columns[b])
    for j in range(tile_row.shape[0]):
        tile_row[j : j + 1] = col_ref[homes[j], BLOCKS]


def potentials(row_gathered, gathered, homes):
    width = gathered.shape[3]
    return pl.pallas_call(
        potentials_kernel,
        in_specs=[SCALARS, WHOLE, WHOLE],
        out_specs=[WHOLE] * 3,
        out_shape=[jax.ShapeDtypeStruct((n, width), F32) for n in (BLOCKS, BLOCKS, homes.shape[0])],
        cost_estimate=LIGHT,
        name="potentials",
    )(homes, row_gathered, gathered)


def pick_kernel(ids, table, first, *refs):
    del first
    outs, buf, come, go = refs[:-3], refs[-3], refs[-2], refs[-1]
    groups, tiles = buf.shape[:2]

    def fetch(i, j):
        return pltpu.make_async_copy(table.at[ids[i, j]], buf.at[i, j], come.at[i, j])

    for i in range(groups):
        start_all([fetch(i, j) for j in range(tiles)])
    stores = [pltpu.make_async_copy(buf.at[i], outs[i], go.at[i]) for i in range(groups)]
    for i in range(groups):
        wait_all([fetch(i, j) for j in range(tiles)])
        stores[i].start()
    wait_all(stores)


def pick(table, ids, after):
    groups, tiles = ids.shape
    shape = (tiles,) + table.shape[1:]
    return pl.pallas_call(
        pick_kernel,
        in_specs=[SCALARS, ANYWHERE, ANYWHERE],
        out_specs=[ANYWHERE] * groups,
        out_shape=[jax.ShapeDtypeStruct(shape, table.dtype)] * groups,
        scratch_shapes=[
            pltpu.VMEM((groups,) + shape, table.dtype),
            pltpu.SemaphoreType.DMA((groups, tiles)),
            pltpu.SemaphoreType.DMA((groups,)),
        ],
        compiler_params=pltpu.CompilerParams(vmem_limit_bytes=16 << 20),
        cost_estimate=LIGHT,
        name="pick_pieces",
    )(ids, *far([table, after]))


def posterior_kernel(scale, count, tile_tgt, places, *refs):
    x_hbm, refs = refs[:count], refs[count:]
    y_hbm, r_ref, c_ref, o_hbm, x, y, o, x_sem, y_sem, o_sem = refs
    tiles, width, depth = x.shape
    groups = count // len(PARTS)
    piece = width // groups
    cuts = o_sem.shape[1]
    rows = width // cuts

    def x_copies(j):
        copies = []
        for part in range(len(PARTS)):
            for p in range(groups):
                src = x_hbm[part * groups + p]
                at = places[p] * piece + sum(x_hbm[earlier * groups].shape[1] for earlier in range(part))
                rows = pl.ds(pl.multiple_of(at, 16), src.shape[1])
                copies.append(pltpu.make_async_copy(src.at[j], x.at[j, rows], x_sem.at[j, part, p]))
        return copies

    def y_copy(j):
        return pltpu.make_async_copy(y_hbm.at[tile_tgt[j]], y.at[j], y_sem.at[j])

    def o_copy(j, q):
        at = pl.ds(q * rows, rows)
        return pltpu.make_async_copy(o.at[j, at], o_hbm.at[0, 0, j, at], o_sem.at[j, q])

    def fetch(j):
        y_copy(j).start()
        start_all(x_copies(j))

    fetch(0)
    fetch(1)

    def step(j, carry):
        @pl.when(j + 2 < tiles)
        def _():
            fetch(j + 2)

        y_copy(j).wait()
        wait_all(x_copies(j))
        col = c_ref[pl.ds(tile_tgt[j], 1), :]
        for q in range(cuts):
            at = slice(q * rows, (q + 1) * rows)
            row = jnp.broadcast_to(r_ref[pl.ds(j, 1), at], (128, rows)).T
            for start in range(0, width, 256):
                s = lax.dot_general(x[j, at], y[j, start : start + 256], NT, preferred_element_type=F32) * scale
                for g in range(0, 256, 128):
                    cols = slice(start + g, start + g + 128)
                    o[j, at, cols] = s[:, g : g + 128] + row + col[:, cols]
            o_copy(j, q).start()
        return carry

    lax.fori_loop(0, tiles, step, 0)
    for j in range(tiles):
        wait_all([o_copy(j, q) for q in range(cuts)])


def posterior(pieces, places, targets, tile_row, column_pot, tile_tgt):
    tiles, _, depth = pieces[0].shape
    width = targets.shape[1]
    cuts = 2
    return pl.pallas_call(
        functools.partial(posterior_kernel, 2.0 / math.sqrt(depth), len(pieces)),
        in_specs=[SCALARS, SCALARS] + [ANYWHERE] * (len(pieces) + 1) + [WHOLE, WHOLE],
        out_specs=ANYWHERE,
        scratch_shapes=[
            pltpu.VMEM((tiles, width, depth), BF16),
            pltpu.VMEM((tiles, width, depth), BF16),
            pltpu.VMEM((tiles, width, width), F32),
            pltpu.SemaphoreType.DMA((tiles, len(PARTS), len(pieces) // len(PARTS))),
            pltpu.SemaphoreType.DMA((tiles,)),
            pltpu.SemaphoreType.DMA((tiles, cuts)),
        ],
        out_shape=jax.ShapeDtypeStruct((1, 1, tiles, width, width), F32),
        compiler_params=pltpu.CompilerParams(vmem_limit_bytes=54 << 20),
        cost_estimate=LIGHT,
        name="posterior",
    )(tile_tgt, places, *far([*pieces, targets]), tile_row, column_pot)


def swap(x, axis):
    return lax.all_to_all(x, axis, split_axis=0, concat_axis=0, tiled=True)


def torus_pieces(parts, side):
    def shift(x, axis, by):
        def to(i):
            a, b = divmod(i, side)
            a, b = ((a + by) % side, b) if axis == 0 else (a, (b + by) % side)
            return a * side + b

        return lax.ppermute(x, "src", [(i, to(i)) for i in range(side * side)])

    pieces = []
    lines = []
    for route, part in enumerate(parts):
        lines.append(jnp.stack([part] + [shift(part, route, k) for k in range(1, side)]))
    back = [shift(line, 1 - route, 1) for route, line in enumerate(lines)]
    ahead = [shift(line, 1 - route, -1) for route, line in enumerate(lines)]
    mid = side // 2
    for route, line in enumerate(lines):
        far = [shift(back[route][:mid], 1 - route, 1), shift(ahead[route][mid:], 1 - route, -1)]
        pieces += [line, back[route], *far, ahead[route]]
    return pieces


def on_device(source_emb, target_emb, slot_source, slot_target):
    src_blocks, tgt_blocks = source_emb.shape[0], target_emb.shape[0]
    src_count, tgt_count = lax.axis_size("src"), lax.axis_size("tgt")
    own_row, own_col = lax.axis_index("src"), lax.axis_index("tgt")
    tiles = slot_source.shape[2]
    tile_src = slot_source[0, 0]
    tile_tgt = slot_target[0, 0] - own_col * tgt_blocks
    tile_home = tile_src // src_blocks

    cores = 2
    length = tgt_count // cores
    turns = [(far, other) for far in range(length) for other in range(cores)]

    def turned(t, far, other):
        return (t // cores + far) % length * cores + (t % cores + other) % cores

    def turn(x, far, other):
        return lax.ppermute(x, "tgt", [(t, turned(t, far, other)) for t in range(tgt_count)])

    places = jnp.stack([turned(own_col, length - far, other) for far, other in turns])

    whole_blocks = lax.all_gather(source_emb, "tgt", axis=1, tiled=True)
    side = math.isqrt(src_count)
    target_pieces = torus_pieces((target_emb[: tgt_blocks // 2], target_emb[tgt_blocks // 2 :]), side)

    slots = jnp.concatenate([slot_source[0, 0], slot_target[0, 0]])
    slots = jnp.pad(slots, (0, 128 - 2 * tiles))[None, None]
    column_slots = swap(jnp.broadcast_to(slots, (src_count, 1, 128)), "src")[:, 0]
    named_src = column_slots[:, :tiles].reshape(-1) - own_row * src_blocks
    named_tgt = column_slots[:, tiles : 2 * tiles].reshape(-1) - own_col * tgt_blocks
    named = jnp.any(
        (named_src[:, None, None] == jnp.arange(src_blocks)[None, :, None])
        & (named_tgt[:, None, None] == jnp.arange(tgt_blocks)[None, None, :]),
        axis=0,
    ).astype(jnp.int32)
    plan_column = home_plan(column_slots[:, :tiles], own_row, src_blocks)

    aimed = jnp.stack([turned(own_col, far, other) for far, other in turns])
    slot_row = jnp.pad(tile_src.astype(F32), (0, target_emb.shape[1] * src_count - tiles))[None]
    shards = cut(source_emb, [whole_blocks, named] + target_pieces)
    tables = [lax.all_gather(shard, "src", axis=0, tiled=True) for shard in shards]
    where = jnp.stack([own_row // side, own_row % side])
    weights, sums, targets = score_weights(whole_blocks, target_pieces, where, named, slot_row, tgt_count, side, shards)
    pieces = [[None] * len(turns) for _ in PARTS]
    windows = [[(0, [0, 2, 6, 3, 7, 4])], [(0, [1, 5]), (1, [0, 2, 6, 4])], [(1, [1, 3, 7, 5])]]
    for iteration, window in enumerate(windows):
        if iteration:
            sums = weighted_sums(row_kernel, gathered, weights, tgt_count, after=picked)
            sums = gate(sums, arrived)
        row_gathered = swap(sums, "tgt")
        if not iteration:
            aims = row_gathered[:, BLOCKS, 0, :tiles].astype(jnp.int32)[aimed]
        picked, arrived = [], []
        for number, (part, chosen) in enumerate(window):
            if number:
                sums = weighted_sums(column_kernel, row_gathered, weights, src_count)
            taken = pick(tables[part], aims[jnp.array(chosen)], sums if number else row_gathered)
            for x, i in zip(taken, chosen):
                pieces[part][i] = turn(x, *turns[i]) if i else x
                picked.append(x)
                arrived.append(pieces[part][i])
        if iteration == ITERS - 1:
            sums = weighted_sums(last_column_kernel, row_gathered, weights, src_count, after=[plan_column, *picked])
        elif len(window) == 1:
            sums = weighted_sums(column_kernel, row_gathered, weights, src_count, after=picked)
        gathered = swap(sums, "src")
    pieces = pieces[0] + pieces[1]

    row_pot, column_pot, tile_row = potentials(row_gathered, gathered, tile_home)

    def unfinished(carry):
        return carry[0]

    def redo(carry):
        zeros = [jnp.zeros_like(carry[1]), jnp.zeros_like(carry[3])]
        scores = posterior(pieces, places, targets, zeros[1], zeros[0], tile_tgt)[0, 0]
        potentials = log_domain(scores, tile_home, tile_tgt, plan_column, src_blocks, tgt_blocks)
        return (jnp.zeros((), jnp.bool_),) + potentials

    out_of_range = jnp.isnan(row_pot[0, 0])
    carry = (out_of_range, column_pot, row_pot, tile_row)
    _, column_pot, row_pot, tile_row = lax.while_loop(unfinished, redo, carry)
    log_post = posterior(pieces, places, targets, tile_row, column_pot, tile_tgt)
    return (log_post, row_pot, column_pot)


def solution(mesh):
    placed = (
        P("src", "tgt", None),
        P("tgt", "src", None),
        P("src", "tgt", None),
        P("src", "tgt", None),
    )
    return jax.shard_map(
        on_device,
        mesh=mesh,
        in_specs=placed,
        out_specs=(P("src", "tgt", None, None, None), P("src", None), P("tgt", None)),
        check_vma=False,
    )
```

```python
import functools
import math

import jax
import jax.numpy as jnp
from jax import lax
from jax.experimental import pallas as pl
from jax.experimental.pallas import tpu as pltpu
from jax.sharding import PartitionSpec as P

ITERS = 3
NEG = -1e30
F32, BF16 = jnp.float32, jnp.bfloat16
LIMIT = 20.0
ROWS = 512
BLOCKS = 4
PARTS = (64, 64)
LIGHT = pl.CostEstimate(flops=0, bytes_accessed=1024, transcendentals=0)
NT = (((1,), (1,)), ((), ()))


def combine_blocks(maxima, totals, labels, groups):
    matches = labels[:, None] == jnp.arange(groups)[None, :]
    largest = jnp.max(jnp.where(matches[:, :, None], maxima[:, None, :], NEG), axis=0)
    diffs = jnp.where(matches[:, :, None], maxima[:, None, :] - largest[None, :, :], NEG)
    scaled = jnp.where(matches[:, :, None], totals[:, None, :] * jnp.exp(diffs), 0.0)
    return (largest, jnp.sum(scaled, axis=0))


def home_plan(slot_ids, own_row, per_row):
    matched = slot_ids // per_row == own_row
    chosen = jnp.sum(jnp.where(matched, slot_ids % per_row, 0), axis=1)
    return jnp.where(jnp.any(matched, axis=1), chosen, -1)


def select_rows(table, plan):
    picked = jnp.take(table, jnp.maximum(plan, 0), axis=0, mode="clip")
    present = (plan >= 0).reshape((-1,) + (1,) * (table.ndim - 1))
    return jnp.where(present, picked, jnp.zeros((), table.dtype))


def log_domain(scores, tile_home, tile_tgt, plan_column, src_blocks, tgt_blocks):
    block_rows = scores.shape[1]
    src_count = lax.axis_size("src")

    def iterate(_, carry):
        column_pot, _, _ = carry
        tile_col = jnp.take(column_pot, tile_tgt, axis=0)
        shifted = scores + tile_col[:, None, :]
        row_max = jnp.max(shifted, axis=2)
        row_sum = jnp.sum(jnp.exp(shifted - row_max[:, :, None]), axis=2)
        send_max, send_sum = combine_blocks(row_max, row_sum, tile_home, src_count)
        local_max, local_sum = combine_blocks(swap(send_max, "src"), swap(send_sum, "src"), plan_column, src_blocks)
        largest = lax.pmax(local_max, "tgt")
        summed = lax.psum(local_sum * jnp.exp(local_max - largest), "tgt")
        row_pot = -(largest + jnp.log(summed))
        tile_row = jnp.take(swap(select_rows(row_pot, plan_column), "src"), tile_home, axis=0)
        shifted = scores + tile_row[:, :, None]
        col_max = jnp.max(shifted, axis=1)
        col_sum = jnp.sum(jnp.exp(shifted - col_max[:, None, :]), axis=1)
        local_max, local_sum = combine_blocks(col_max, col_sum, tile_tgt, tgt_blocks)
        largest = lax.pmax(local_max, "src")
        summed = lax.psum(local_sum * jnp.exp(local_max - largest), "src")
        return (-(largest + jnp.log(summed)), row_pot, tile_row)

    init = (
        jnp.zeros((tgt_blocks, block_rows), F32),
        jnp.zeros((src_blocks, block_rows), F32),
        jnp.zeros((scores.shape[0], block_rows), F32),
    )
    return lax.fori_loop(0, ITERS, iterate, init)


def stack3(x):
    hi = x.astype(BF16).astype(F32)
    mid = (x - hi).astype(BF16).astype(F32)
    low = x - hi - mid
    row = lax.broadcasted_iota(jnp.int32, (16, x.shape[1]), 0)
    parts = [jnp.broadcast_to(p, row.shape) for p in (hi, mid, low)]
    return jnp.where(row == 0, parts[0], jnp.where(row == 1, parts[1], jnp.where(row == 2, parts[2], 0.0))).astype(BF16)


def lane_totals(lanes):
    ones = jnp.ones((8, 128), F32)
    return lax.dot_general(ones, lanes, NT, preferred_element_type=F32, precision=lax.Precision.HIGHEST)[0:1]


def put(o_ref, block, cols, out):
    o_ref[:, block, :, cols] = jnp.broadcast_to(out[None], (o_ref.shape[0],) + out.shape)


def all_within(x, low, high):
    return jnp.min(jnp.where((x >= low) & (x <= high), 1.0, 0.0)) > 0.0


def start_all(copies):
    for copy in copies:
        copy.start()


def wait_all(copies):
    for copy in copies:
        copy.wait()


def scores_kernel(scale, side, named, where, extra, x_hbm, *refs):
    pieces, refs = refs[:10], refs[-12:]
    k_hbm, sum_ref, ratio_ref, targets_hbm, x, y, k_out, lowest, x_sem, y_sem, k_sem, leave = refs
    blocks, width, _ = y.shape
    rows = k_out.shape[1]
    half = blocks // 2
    mid = side // 2
    small = width // (side * side)

    def target_copy(route, far, near):
        first = lax.rem(where[route] - near + side, side)
        second = lax.rem(where[1 - route] - far + side, side)
        at = (first * side + second if route == 0 else second * side + first) * small
        stage, entry = far, near
        if far >= mid:
            stage, entry = (far, near) if far == mid and near < mid else (far + 1, near - mid if far == mid else near)
        return pltpu.make_async_copy(
            pieces[route * (side + 1) + stage].at[entry],
            y.at[pl.ds(route * half, half), pl.ds(pl.multiple_of(at, small), small), :],
            y_sem.at[route, far, near],
        )

    def target_copies(route):
        return [target_copy(route, far, near) for far in range(side) for near in range(side)]

    def source_copy(b):
        return pltpu.make_async_copy(x_hbm.at[b], x.at[b], x_sem.at[b])

    def out_copy(i, slot):
        at = pl.ds(pl.multiple_of(i * rows, rows), rows)
        return pltpu.make_async_copy(k_out.at[slot], k_hbm.at[at], k_sem.at[slot])

    start_all(target_copies(0))
    source_copy(0).start()
    start_all(target_copies(1))
    start_all([source_copy(b) for b in range(1, blocks)])
    lowest[...] = jnp.ones_like(lowest)
    put(sum_ref, blocks, slice(None), extra[...])
    wait_all(target_copies(0) + target_copies(1))
    whole_targets = pltpu.make_async_copy(y, targets_hbm, leave)
    whole_targets.start()
    per = width // rows

    def step(i, carry):
        b, part, slot = i // per, lax.rem(i, per), lax.rem(i, 2)

        @pl.when(part == 0)
        def _():
            source_copy(b).wait()

        @pl.when(i >= 2)
        def _():
            out_copy(i - 2, slot).wait()

        low = lowest[...]
        lanes = jnp.zeros((rows, 128), F32)
        rounded = jnp.zeros((rows, 128), F32)
        here = x[b, pl.ds(pl.multiple_of(part * rows, rows), rows), :]
        for c in range(blocks):
            s = lax.dot_general(here, y[c], NT, preferred_element_type=F32)
            e = jnp.exp2(s * scale)
            k = e.astype(BF16)
            is_named = named[b, c] > 0
            k_out[slot, :, c * width : (c + 1) * width] = jnp.where(is_named, k, jnp.zeros_like(k))
            acc, kept, least = e[:, :128], k[:, :128].astype(F32), k[:, :128]
            for g in range(128, width, 128):
                acc = acc + e[:, g : g + 128]
                kept = kept + k[:, g : g + 128].astype(F32)
                least = jnp.minimum(least, k[:, g : g + 128])
            lanes = lanes + jnp.where(is_named, acc, 0.0)
            rounded = rounded + jnp.where(is_named, kept, 0.0)
            low = jnp.minimum(low, jnp.min(least.reshape(rows // 16, 16, 128), axis=0))
        lowest[...] = low
        out_copy(i, slot).start()
        total = lane_totals(lanes)
        fine = (jnp.min(low.astype(F32)) > math.exp(-LIMIT)) & all_within(total, 0.0, math.exp(LIMIT))
        at = pl.ds(pl.multiple_of(part * rows, rows), rows)
        put(sum_ref, b, at, jnp.where(fine, total, jnp.nan))
        low_sum = lane_totals(rounded)
        ratio_ref[b, :, at] = jnp.where(low_sum > 0.0, total / low_sum, 1.0)
        return carry

    lax.fori_loop(0, blocks * per, step, 0)
    for i in (blocks * per - 2, blocks * per - 1):
        out_copy(i, i % 2).wait()
    whole_targets.wait()


ANYWHERE = pl.BlockSpec(memory_space=pl.ANY)
SCALARS = pl.BlockSpec(memory_space=pltpu.SMEM)
WHOLE = pl.BlockSpec(memory_space=pltpu.VMEM)


def far(arrays):
    return [pltpu.with_memory_space_constraint(x, pltpu.HBM) for x in arrays]


def score_weights(x, pieces, where, named, extra, copies, side, after):
    blocks, width, depth = x.shape
    n = blocks * width
    return pl.pallas_call(
        functools.partial(scores_kernel, 2.0 / math.sqrt(depth) * math.log2(math.e), side),
        in_specs=[SCALARS, SCALARS, WHOLE] + [ANYWHERE] * (1 + len(pieces) + len(after)),
        out_specs=[ANYWHERE, WHOLE, WHOLE, ANYWHERE],
        scratch_shapes=[
            pltpu.VMEM((blocks, width, depth), BF16),
            pltpu.VMEM((blocks, width, depth), BF16),
            pltpu.VMEM((2, ROWS, n), BF16),
            pltpu.VMEM((16, 128), BF16),
            pltpu.SemaphoreType.DMA((blocks,)),
            pltpu.SemaphoreType.DMA((2, side, side)),
            pltpu.SemaphoreType.DMA((2,)),
            pltpu.SemaphoreType.DMA,
        ],
        out_shape=[
            jax.ShapeDtypeStruct((n, n), BF16),
            jax.ShapeDtypeStruct((copies, blocks + 1, 1, width), F32),
            jax.ShapeDtypeStruct((blocks, 1, width), F32),
            jax.ShapeDtypeStruct((blocks, width, depth), BF16),
        ],
        compiler_params=pltpu.CompilerParams(vmem_limit_bytes=44 << 20),
        cost_estimate=LIGHT,
        name="score_weights",
    )(named, where, extra, *far([x, *pieces, *after]))


def inverse_parts(g_ref, low, high):
    total = jnp.sum(g_ref[:, :BLOCKS], axis=0)
    fine = all_within(total, low, high)
    return [1.0 / total[b] for b in range(total.shape[0])], jnp.where(fine, 0.0, jnp.nan)


def column_kernel(g_ref, ratio, k_hbm, *refs):
    columns(g_ref, ratio, k_hbm, *refs[-3:])


def last_column_kernel(g_ref, ratio, k_hbm, plan, *refs):
    o_ref, k, sem, logs = refs[-4:]
    total = jnp.sum(g_ref[:, :BLOCKS], axis=0)
    logs[...] = -jnp.log(total)
    for s in range(o_ref.shape[0]):
        o_ref[s, total.shape[0]] = logs[jnp.maximum(plan[s], 0)]
    columns(g_ref, ratio, k_hbm, o_ref, k, sem)


def columns(g_ref, ratio, k_hbm, o_ref, k, sem):
    parts, n, cols = k.shape
    copies = [pltpu.make_async_copy(k_hbm.at[:, pl.ds(j * cols, cols)], k.at[j], sem.at[j]) for j in range(parts)]
    start_all(copies)
    inv, spoil = inverse_parts(g_ref, 1e-38, 1e38)
    blocks, width = len(inv), inv[0].shape[1]
    lhs = [stack3(v * ratio[b]) for b, v in enumerate(inv)]
    per = width // cols
    for j in range(parts):
        copies[j].wait()
        acc = jnp.zeros((16, cols), F32)
        for b in range(blocks):
            acc = acc + jnp.dot(lhs[b], k[j, b * width : (b + 1) * width, :], preferred_element_type=F32)
        start = (j % per) * cols
        put(o_ref, j // per, slice(start, start + cols), acc[0:1] + acc[1:2] + acc[2:3] + spoil)


def row_kernel(g_ref, ratio, k_hbm, *refs):
    o_ref, k, sem = refs[-3:]
    parts, rows, n = k.shape
    copies = [pltpu.make_async_copy(k_hbm.at[pl.ds(j * rows, rows)], k.at[j], sem.at[j]) for j in range(parts)]
    start_all(copies)
    inv, spoil = inverse_parts(g_ref, math.exp(-LIMIT), math.exp(LIMIT))
    blocks, width = len(inv), inv[0].shape[1]
    half = blocks // 2
    lhs = [stack3(v) for v in inv[:half]]
    per = width // rows
    for j in range(parts):
        copies[j].wait()
        acc = jnp.zeros((16, rows), F32)
        for c in range(half):
            acc = acc + lax.dot_general(
                lhs[c], k[j, :, c * width : (c + 1) * width], NT, preferred_element_type=F32
            )
        lanes = jnp.zeros((rows, 128), F32)
        for c in range(half, blocks):
            for g in range(0, width, 128):
                at = c * width + g
                lanes = lanes + k[j, :, at : at + 128].astype(F32) * inv[c][:, g : g + 128]
        start = (j % per) * rows
        at = slice(start, start + rows)
        out = (acc[0:1] + acc[1:2] + acc[2:3] + lane_totals(lanes)) * ratio[j // per, :, at]
        put(o_ref, j // per, at, out + spoil)


def weighted_sums(kernel, gathered, ratio, k, copies, after=()):
    n = k.shape[0]
    blocks, width = BLOCKS, gathered.shape[3]
    parts = n // ROWS
    last = kernel is last_column_kernel
    shape = (parts, ROWS, n) if kernel is row_kernel else (parts, n, ROWS)
    return pl.pallas_call(
        kernel,
        in_specs=[WHOLE, WHOLE, ANYWHERE] + [SCALARS] * last + [ANYWHERE] * (len(after) - last),
        out_specs=WHOLE,
        out_shape=jax.ShapeDtypeStruct((copies, blocks + last, 1, width), F32),
        scratch_shapes=[pltpu.VMEM(shape, BF16), pltpu.SemaphoreType.DMA((parts,))]
        + ([pltpu.VMEM((blocks, 1, width), F32)] if last else []),
        compiler_params=pltpu.CompilerParams(vmem_limit_bytes=44 << 20),
        cost_estimate=LIGHT,
        name="row_sums" if kernel is row_kernel else "column_sums",
    )(gathered, ratio, *far([k]), *after[:last], *far(after[last:]))


def cut_kernel(x_ref, *refs):
    start = 0
    for out in refs[-len(PARTS) :]:
        rows = out.shape[1]
        out[...] = x_ref[:, start : start + rows, :]
        start += rows


def cut(x, after):
    whole = x.shape[1] // sum(PARTS)
    return pl.pallas_call(
        cut_kernel,
        in_specs=[WHOLE] + [ANYWHERE] * len(after),
        out_specs=[WHOLE] * len(PARTS),
        out_shape=[jax.ShapeDtypeStruct((x.shape[0], rows * whole, x.shape[2]), x.dtype) for rows in PARTS],
        compiler_params=pltpu.CompilerParams(vmem_limit_bytes=16 << 20),
        cost_estimate=LIGHT,
        name="cut_rows",
    )(x, *far(after))


def gate_kernel(x_ref, *refs):
    refs[-1][...] = jnp.broadcast_to(x_ref[...], refs[-1].shape)


def gate(x, copies, after):
    return pl.pallas_call(
        gate_kernel,
        in_specs=[WHOLE] + [ANYWHERE] * len(after),
        out_specs=WHOLE,
        out_shape=jax.ShapeDtypeStruct((copies,) + x.shape[1:], x.dtype),
        cost_estimate=LIGHT,
        name="gate",
    )(x, *far(after))


def potentials_kernel(homes, row_ref, col_ref, row_pot, column_pot, tile_row):
    rows = jnp.sum(row_ref[:, :BLOCKS], axis=0)
    columns = jnp.sum(col_ref[:, :BLOCKS], axis=0)
    for b in range(BLOCKS):
        row_pot[b : b + 1] = -jnp.log(rows[b])
        column_pot[b : b + 1] = -jnp.log(columns[b])
    for j in range(tile_row.shape[0]):
        tile_row[j : j + 1] = col_ref[homes[j], BLOCKS]


def potentials(row_gathered, gathered, homes):
    width = gathered.shape[3]
    return pl.pallas_call(
        potentials_kernel,
        in_specs=[SCALARS, WHOLE, WHOLE],
        out_specs=[WHOLE] * 3,
        out_shape=[jax.ShapeDtypeStruct((n, width), F32) for n in (BLOCKS, BLOCKS, homes.shape[0])],
        cost_estimate=LIGHT,
        name="potentials",
    )(homes, row_gathered, gathered)


def pick_kernel(ids, table, first, *refs):
    del first
    outs, buf, come, go = refs[:-3], refs[-3], refs[-2], refs[-1]
    groups, tiles = buf.shape[:2]

    def fetch(i, j):
        return pltpu.make_async_copy(table.at[ids[i, j]], buf.at[i, j], come.at[i, j])

    for i in range(groups):
        start_all([fetch(i, j) for j in range(tiles)])
    stores = [pltpu.make_async_copy(buf.at[i], outs[i], go.at[i]) for i in range(groups)]
    for i in range(groups):
        wait_all([fetch(i, j) for j in range(tiles)])
        stores[i].start()
    wait_all(stores)


def pick(table, ids, after):
    groups, tiles = ids.shape
    shape = (tiles,) + table.shape[1:]
    return pl.pallas_call(
        pick_kernel,
        in_specs=[SCALARS, ANYWHERE, ANYWHERE],
        out_specs=[ANYWHERE] * groups,
        out_shape=[jax.ShapeDtypeStruct(shape, table.dtype)] * groups,
        scratch_shapes=[
            pltpu.VMEM((groups,) + shape, table.dtype),
            pltpu.SemaphoreType.DMA((groups, tiles)),
            pltpu.SemaphoreType.DMA((groups,)),
        ],
        compiler_params=pltpu.CompilerParams(vmem_limit_bytes=16 << 20),
        cost_estimate=LIGHT,
        name="pick_pieces",
    )(ids, *far([table]), after)


def posterior_kernel(scale, count, tile_tgt, places, *refs):
    x_hbm, refs = refs[:count], refs[count:]
    y_hbm, r_ref, c_ref, o_hbm, x, y, o, x_sem, y_sem, o_sem = refs
    tiles, width, depth = x.shape
    groups = count // len(PARTS)
    piece = width // groups
    cuts = o_sem.shape[1]
    rows = width // cuts

    def x_copies(j):
        copies = []
        for part in range(len(PARTS)):
            for p in range(groups):
                src = x_hbm[part * groups + p]
                at = places[p] * piece + sum(x_hbm[earlier * groups].shape[1] for earlier in range(part))
                rows = pl.ds(pl.multiple_of(at, 16), src.shape[1])
                copies.append(pltpu.make_async_copy(src.at[j], x.at[j, rows], x_sem.at[j, part, p]))
        return copies

    def y_copy(j):
        return pltpu.make_async_copy(y_hbm.at[tile_tgt[j]], y.at[j], y_sem.at[j])

    def o_copy(j, q):
        at = pl.ds(q * rows, rows)
        return pltpu.make_async_copy(o.at[j, at], o_hbm.at[0, 0, j, at], o_sem.at[j, q])

    def fetch(j):
        y_copy(j).start()
        start_all(x_copies(j))

    fetch(0)
    fetch(1)

    def step(j, carry):
        @pl.when(j + 2 < tiles)
        def _():
            fetch(j + 2)

        y_copy(j).wait()
        wait_all(x_copies(j))
        col = c_ref[pl.ds(tile_tgt[j], 1), :]
        for q in range(cuts):
            at = slice(q * rows, (q + 1) * rows)
            row = jnp.broadcast_to(r_ref[pl.ds(j, 1), at], (128, rows)).T
            for start in range(0, width, 256):
                s = lax.dot_general(x[j, at], y[j, start : start + 256], NT, preferred_element_type=F32) * scale
                for g in range(0, 256, 128):
                    cols = slice(start + g, start + g + 128)
                    o[j, at, cols] = s[:, g : g + 128] + row + col[:, cols]
            o_copy(j, q).start()
        return carry

    lax.fori_loop(0, tiles, step, 0)
    for j in range(tiles):
        wait_all([o_copy(j, q) for q in range(cuts)])


def posterior(pieces, places, targets, tile_row, column_pot, tile_tgt):
    tiles, _, depth = pieces[0].shape
    width = targets.shape[1]
    cuts = 2
    return pl.pallas_call(
        functools.partial(posterior_kernel, 2.0 / math.sqrt(depth), len(pieces)),
        in_specs=[SCALARS, SCALARS] + [ANYWHERE] * (len(pieces) + 1) + [WHOLE, WHOLE],
        out_specs=ANYWHERE,
        scratch_shapes=[
            pltpu.VMEM((tiles, width, depth), BF16),
            pltpu.VMEM((tiles, width, depth), BF16),
            pltpu.VMEM((tiles, width, width), F32),
            pltpu.SemaphoreType.DMA((tiles, len(PARTS), len(pieces) // len(PARTS))),
            pltpu.SemaphoreType.DMA((tiles,)),
            pltpu.SemaphoreType.DMA((tiles, cuts)),
        ],
        out_shape=jax.ShapeDtypeStruct((1, 1, tiles, width, width), F32),
        compiler_params=pltpu.CompilerParams(vmem_limit_bytes=54 << 20),
        cost_estimate=LIGHT,
        name="posterior",
    )(tile_tgt, places, *far([*pieces, targets]), tile_row, column_pot)


def swap(x, axis):
    return lax.all_to_all(x, axis, split_axis=0, concat_axis=0, tiled=True)


def torus_pieces(parts, side):
    def shift(x, axis, by):
        def to(i):
            a, b = divmod(i, side)
            a, b = ((a + by) % side, b) if axis == 0 else (a, (b + by) % side)
            return a * side + b

        return lax.ppermute(x, "src", [(i, to(i)) for i in range(side * side)])

    pieces = []
    lines = []
    for route, part in enumerate(parts):
        lines.append(jnp.stack([part] + [shift(part, route, k) for k in range(1, side)]))
    back = [shift(line, 1 - route, 1) for route, line in enumerate(lines)]
    ahead = [shift(line, 1 - route, -1) for route, line in enumerate(lines)]
    mid = side // 2
    for route, line in enumerate(lines):
        far = [shift(back[route][:mid], 1 - route, 1), shift(ahead[route][mid:], 1 - route, -1)]
        pieces += [line, back[route], *far, ahead[route]]
    return pieces


def on_device(source_emb, target_emb, slot_source, slot_target):
    src_blocks, tgt_blocks = source_emb.shape[0], target_emb.shape[0]
    src_count, tgt_count = lax.axis_size("src"), lax.axis_size("tgt")
    own_row, own_col = lax.axis_index("src"), lax.axis_index("tgt")
    tiles = slot_source.shape[2]
    tile_src = slot_source[0, 0]
    tile_tgt = slot_target[0, 0] - own_col * tgt_blocks
    tile_home = tile_src // src_blocks

    cores = 2
    length = tgt_count // cores
    turns = [(far, other) for far in range(length) for other in range(cores)]

    def turned(t, far, other):
        return (t // cores + far) % length * cores + (t % cores + other) % cores

    def turn(x, far, other):
        return lax.ppermute(x, "tgt", [(t, turned(t, far, other)) for t in range(tgt_count)])

    places = jnp.stack([turned(own_col, length - far, other) for far, other in turns])

    whole_blocks = lax.all_gather(source_emb, "tgt", axis=1, tiled=True)
    side = math.isqrt(src_count)
    target_pieces = torus_pieces((target_emb[: tgt_blocks // 2], target_emb[tgt_blocks // 2 :]), side)

    slots = jnp.concatenate([slot_source[0, 0], slot_target[0, 0]])
    slots = jnp.pad(slots, (0, 128 - 2 * tiles))[None, None]
    column_slots = swap(jnp.broadcast_to(slots, (src_count, 1, 128)), "src")[:, 0]
    named_src = column_slots[:, :tiles].reshape(-1) - own_row * src_blocks
    named_tgt = column_slots[:, tiles : 2 * tiles].reshape(-1) - own_col * tgt_blocks
    named = jnp.any(
        (named_src[:, None, None] == jnp.arange(src_blocks)[None, :, None])
        & (named_tgt[:, None, None] == jnp.arange(tgt_blocks)[None, None, :]),
        axis=0,
    ).astype(jnp.int32)
    plan_column = home_plan(column_slots[:, :tiles], own_row, src_blocks)

    aimed = jnp.stack([turned(own_col, far, other) for far, other in turns])
    slot_row = jnp.pad(tile_src.astype(F32), (0, target_emb.shape[1] * src_count - tiles))[None]
    shards = cut(source_emb, [whole_blocks, named] + target_pieces)
    tables = [lax.all_gather(shard, "src", axis=0, tiled=True) for shard in shards]
    where = jnp.stack([own_row // side, own_row % side])
    weights, sums, ratio, targets = score_weights(whole_blocks, target_pieces, where, named, slot_row, tgt_count, side, shards)
    pieces = [[None] * len(turns) for _ in PARTS]
    windows = [[(0, [0, 2, 6, 3, 7, 4])], [(0, [1, 5]), (1, [0, 2, 6, 4])], [(1, [1, 3, 7, 5])]]
    for iteration, window in enumerate(windows):
        if iteration:
            sums = weighted_sums(row_kernel, gathered, ratio, weights, 1, after=picked)
            sums = gate(sums, tgt_count, arrived)
        row_gathered = swap(sums, "tgt")
        if not iteration:
            aims = row_gathered[:, BLOCKS, 0, :tiles].astype(jnp.int32)[aimed]
        picked, arrived = [], []
        for number, (part, chosen) in enumerate(window):
            if number:
                sums = weighted_sums(column_kernel, row_gathered, ratio, weights, src_count, after=picked)
            taken = pick(tables[part], aims[jnp.array(chosen)], sums if number else row_gathered)
            for x, i in zip(taken, chosen):
                pieces[part][i] = turn(x, *turns[i]) if i else x
                picked.append(x)
                arrived.append(pieces[part][i])
        if iteration == ITERS - 1:
            sums = weighted_sums(last_column_kernel, row_gathered, ratio, weights, src_count, after=[plan_column, *picked])
        elif len(window) == 1:
            sums = weighted_sums(column_kernel, row_gathered, ratio, weights, src_count, after=picked)
        gathered = swap(sums, "src")
    pieces = pieces[0] + pieces[1]

    row_pot, column_pot, tile_row = potentials(row_gathered, gathered, tile_home)

    def unfinished(carry):
        return carry[0]

    def redo(carry):
        zeros = [jnp.zeros_like(carry[1]), jnp.zeros_like(carry[3])]
        scores = posterior(pieces, places, targets, zeros[1], zeros[0], tile_tgt)[0, 0]
        potentials = log_domain(scores, tile_home, tile_tgt, plan_column, src_blocks, tgt_blocks)
        return (jnp.zeros((), jnp.bool_),) + potentials

    out_of_range = jnp.isnan(row_pot[0, 0])
    carry = (out_of_range, column_pot, row_pot, tile_row)
    _, column_pot, row_pot, tile_row = lax.while_loop(unfinished, redo, carry)
    log_post = posterior(pieces, places, targets, tile_row, column_pot, tile_tgt)
    return (log_post, row_pot, column_pot)


def solution(mesh):
    placed = (
        P("src", "tgt", None),
        P("tgt", "src", None),
        P("src", "tgt", None),
        P("src", "tgt", None),
    )
    return jax.shard_map(
        on_device,
        mesh=mesh,
        in_specs=placed,
        out_specs=(P("src", "tgt", None, None, None), P("src", None), P("tgt", None)),
        check_vma=False,
    )
```

```python
import functools
import math

import jax
import jax.numpy as jnp
from jax import lax
from jax.experimental import pallas as pl
from jax.experimental.pallas import tpu as pltpu
from jax.sharding import PartitionSpec as P

ITERS = 3
NEG = -1e30
F32, BF16 = jnp.float32, jnp.bfloat16
LIMIT = 20.0
ROWS = 512
BLOCKS = 4
PARTS = (64, 64)
LIGHT = pl.CostEstimate(flops=0, bytes_accessed=1024, transcendentals=0)
NT = (((1,), (1,)), ((), ()))


def combine_blocks(maxima, totals, labels, groups):
    matches = labels[:, None] == jnp.arange(groups)[None, :]
    largest = jnp.max(jnp.where(matches[:, :, None], maxima[:, None, :], NEG), axis=0)
    diffs = jnp.where(matches[:, :, None], maxima[:, None, :] - largest[None, :, :], NEG)
    scaled = jnp.where(matches[:, :, None], totals[:, None, :] * jnp.exp(diffs), 0.0)
    return (largest, jnp.sum(scaled, axis=0))


def home_plan(slot_ids, own_row, per_row):
    matched = slot_ids // per_row == own_row
    chosen = jnp.sum(jnp.where(matched, slot_ids % per_row, 0), axis=1)
    return jnp.where(jnp.any(matched, axis=1), chosen, -1)


def select_rows(table, plan):
    picked = jnp.take(table, jnp.maximum(plan, 0), axis=0, mode="clip")
    present = (plan >= 0).reshape((-1,) + (1,) * (table.ndim - 1))
    return jnp.where(present, picked, jnp.zeros((), table.dtype))


def log_domain(scores, tile_home, tile_tgt, plan_column, src_blocks, tgt_blocks):
    block_rows = scores.shape[1]
    src_count = lax.axis_size("src")

    def iterate(_, carry):
        column_pot, _, _ = carry
        tile_col = jnp.take(column_pot, tile_tgt, axis=0)
        shifted = scores + tile_col[:, None, :]
        row_max = jnp.max(shifted, axis=2)
        row_sum = jnp.sum(jnp.exp(shifted - row_max[:, :, None]), axis=2)
        send_max, send_sum = combine_blocks(row_max, row_sum, tile_home, src_count)
        local_max, local_sum = combine_blocks(swap(send_max, "src"), swap(send_sum, "src"), plan_column, src_blocks)
        largest = lax.pmax(local_max, "tgt")
        summed = lax.psum(local_sum * jnp.exp(local_max - largest), "tgt")
        row_pot = -(largest + jnp.log(summed))
        tile_row = jnp.take(swap(select_rows(row_pot, plan_column), "src"), tile_home, axis=0)
        shifted = scores + tile_row[:, :, None]
        col_max = jnp.max(shifted, axis=1)
        col_sum = jnp.sum(jnp.exp(shifted - col_max[:, None, :]), axis=1)
        local_max, local_sum = combine_blocks(col_max, col_sum, tile_tgt, tgt_blocks)
        largest = lax.pmax(local_max, "src")
        summed = lax.psum(local_sum * jnp.exp(local_max - largest), "src")
        return (-(largest + jnp.log(summed)), row_pot, tile_row)

    init = (
        jnp.zeros((tgt_blocks, block_rows), F32),
        jnp.zeros((src_blocks, block_rows), F32),
        jnp.zeros((scores.shape[0], block_rows), F32),
    )
    return lax.fori_loop(0, ITERS, iterate, init)


def stack3(x):
    hi = x.astype(BF16).astype(F32)
    mid = (x - hi).astype(BF16).astype(F32)
    low = x - hi - mid
    row = lax.broadcasted_iota(jnp.int32, (16, x.shape[1]), 0)
    parts = [jnp.broadcast_to(p, row.shape) for p in (hi, mid, low)]
    return jnp.where(row == 0, parts[0], jnp.where(row == 1, parts[1], jnp.where(row == 2, parts[2], 0.0))).astype(BF16)


def lane_totals(lanes):
    ones = jnp.ones((8, 128), F32)
    return lax.dot_general(ones, lanes, NT, preferred_element_type=F32, precision=lax.Precision.HIGHEST)[0:1]


def put(o_ref, block, cols, out):
    o_ref[:, block, :, cols] = jnp.broadcast_to(out[None], (o_ref.shape[0],) + out.shape)


def all_within(x, low, high):
    return jnp.min(jnp.where((x >= low) & (x <= high), 1.0, 0.0)) > 0.0


def start_all(copies):
    for copy in copies:
        copy.start()


def wait_all(copies):
    for copy in copies:
        copy.wait()


def scores_kernel(scale, side, named, where, extra, x_hbm, *refs):
    pieces, refs = refs[:10], refs[-12:]
    k_hbm, sum_ref, ratio_ref, targets_hbm, x, y, k_out, lowest, x_sem, y_sem, k_sem, leave = refs
    blocks, width, _ = y.shape
    rows = k_out.shape[1]
    half = blocks // 2
    mid = side // 2
    small = width // (side * side)

    def target_copy(route, far, near):
        first = lax.rem(where[route] - near + side, side)
        second = lax.rem(where[1 - route] - far + side, side)
        at = (first * side + second if route == 0 else second * side + first) * small
        stage, entry = far, near
        if far >= mid:
            stage, entry = (far, near) if far == mid and near < mid else (far + 1, near - mid if far == mid else near)
        return pltpu.make_async_copy(
            pieces[route * (side + 1) + stage].at[entry],
            y.at[pl.ds(route * half, half), pl.ds(pl.multiple_of(at, small), small), :],
            y_sem.at[route, far, near],
        )

    def target_copies(route):
        return [target_copy(route, far, near) for far in range(side) for near in range(side)]

    def source_copy(b):
        return pltpu.make_async_copy(x_hbm.at[b], x.at[b], x_sem.at[b])

    def out_copy(i, slot):
        at = pl.ds(pl.multiple_of(i * rows, rows), rows)
        return pltpu.make_async_copy(k_out.at[slot], k_hbm.at[at], k_sem.at[slot])

    start_all(target_copies(0))
    source_copy(0).start()
    start_all(target_copies(1))
    start_all([source_copy(b) for b in range(1, blocks)])
    lowest[...] = jnp.ones_like(lowest)
    put(sum_ref, blocks, slice(None), extra[...])
    wait_all(target_copies(0) + target_copies(1))
    whole_targets = pltpu.make_async_copy(y, targets_hbm, leave)
    whole_targets.start()
    per = width // rows

    def step(i, carry):
        b, part, slot = i // per, lax.rem(i, per), lax.rem(i, 2)

        @pl.when(part == 0)
        def _():
            source_copy(b).wait()

        @pl.when(i >= 2)
        def _():
            out_copy(i - 2, slot).wait()

        low = lowest[...]
        lanes = jnp.zeros((rows, 128), F32)
        rounded = jnp.zeros((rows, 128), F32)
        here = x[b, pl.ds(pl.multiple_of(part * rows, rows), rows), :]
        for c in range(blocks):
            s = lax.dot_general(here, y[c], NT, preferred_element_type=F32)
            e = jnp.exp2(s * scale)
            k = e.astype(BF16)
            is_named = named[b, c] > 0
            k_out[slot, :, c * width : (c + 1) * width] = jnp.where(is_named, k, jnp.zeros_like(k))
            acc, kept, least = e[:, :128], k[:, :128].astype(F32), k[:, :128]
            for g in range(128, width, 128):
                acc = acc + e[:, g : g + 128]
                kept = kept + k[:, g : g + 128].astype(F32)
                least = jnp.minimum(least, k[:, g : g + 128])
            lanes = lanes + jnp.where(is_named, acc, 0.0)
            rounded = rounded + jnp.where(is_named, kept, 0.0)
            low = jnp.minimum(low, jnp.min(least.reshape(rows // 16, 16, 128), axis=0))
        lowest[...] = low
        out_copy(i, slot).start()
        total = lane_totals(lanes)
        fine = (jnp.min(low.astype(F32)) > math.exp(-LIMIT)) & all_within(total, 0.0, math.exp(LIMIT))
        at = pl.ds(pl.multiple_of(part * rows, rows), rows)
        put(sum_ref, b, at, jnp.where(fine, total, jnp.nan))
        low_sum = lane_totals(rounded)
        ratio_ref[b, :, at] = jnp.where(low_sum > 0.0, total / low_sum, 1.0)
        return carry

    lax.fori_loop(0, blocks * per, step, 0)
    for i in (blocks * per - 2, blocks * per - 1):
        out_copy(i, i % 2).wait()
    whole_targets.wait()


ANYWHERE = pl.BlockSpec(memory_space=pl.ANY)
SCALARS = pl.BlockSpec(memory_space=pltpu.SMEM)
WHOLE = pl.BlockSpec(memory_space=pltpu.VMEM)


def far(arrays):
    return [pltpu.with_memory_space_constraint(x, pltpu.HBM) for x in arrays]


def score_weights(x, pieces, where, named, extra, copies, side, after):
    blocks, width, depth = x.shape
    n = blocks * width
    return pl.pallas_call(
        functools.partial(scores_kernel, 2.0 / math.sqrt(depth) * math.log2(math.e), side),
        in_specs=[SCALARS, SCALARS, WHOLE] + [ANYWHERE] * (1 + len(pieces) + len(after)),
        out_specs=[ANYWHERE, WHOLE, WHOLE, ANYWHERE],
        scratch_shapes=[
            pltpu.VMEM((blocks, width, depth), BF16),
            pltpu.VMEM((blocks, width, depth), BF16),
            pltpu.VMEM((2, ROWS, n), BF16),
            pltpu.VMEM((16, 128), BF16),
            pltpu.SemaphoreType.DMA((blocks,)),
            pltpu.SemaphoreType.DMA((2, side, side)),
            pltpu.SemaphoreType.DMA((2,)),
            pltpu.SemaphoreType.DMA,
        ],
        out_shape=[
            jax.ShapeDtypeStruct((n, n), BF16),
            jax.ShapeDtypeStruct((copies, blocks + 1, 1, width), F32),
            jax.ShapeDtypeStruct((blocks, 1, width), F32),
            jax.ShapeDtypeStruct((blocks, width, depth), BF16),
        ],
        compiler_params=pltpu.CompilerParams(vmem_limit_bytes=44 << 20),
        cost_estimate=LIGHT,
        name="score_weights",
    )(named, where, extra, *far([x, *pieces, *after]))


def inverse_parts(g_ref, low, high):
    total = jnp.sum(g_ref[:, :BLOCKS], axis=0)
    fine = all_within(total, low, high)
    return [1.0 / total[b] for b in range(total.shape[0])], jnp.where(fine, 0.0, jnp.nan)


def column_kernel(g_ref, ratio, k_hbm, *refs):
    columns(g_ref, ratio, k_hbm, *refs[-3:])


def last_column_kernel(g_ref, ratio, k_hbm, plan, *refs):
    o_ref, k, sem, logs = refs[-4:]
    total = jnp.sum(g_ref[:, :BLOCKS], axis=0)
    logs[...] = -jnp.log(total)
    for s in range(o_ref.shape[0]):
        o_ref[s, total.shape[0]] = logs[jnp.maximum(plan[s], 0)]
    columns(g_ref, ratio, k_hbm, o_ref, k, sem)


def columns(g_ref, ratio, k_hbm, o_ref, k, sem):
    parts, n, cols = k.shape
    copies = [pltpu.make_async_copy(k_hbm.at[:, pl.ds(j * cols, cols)], k.at[j], sem.at[j]) for j in range(parts)]
    start_all(copies)
    inv, spoil = inverse_parts(g_ref, 1e-38, 1e38)
    blocks, width = len(inv), inv[0].shape[1]
    lhs = [stack3(v * ratio[b]) for b, v in enumerate(inv)]
    per = width // cols
    for j in range(parts):
        copies[j].wait()
        acc = jnp.zeros((16, cols), F32)
        for b in range(blocks):
            acc = acc + jnp.dot(lhs[b], k[j, b * width : (b + 1) * width, :], preferred_element_type=F32)
        start = (j % per) * cols
        put(o_ref, j // per, slice(start, start + cols), acc[0:1] + acc[1:2] + acc[2:3] + spoil)


def row_kernel(g_ref, ratio, k_hbm, *refs):
    o_ref, k, sem = refs[-3:]
    parts, rows, n = k.shape
    copies = [pltpu.make_async_copy(k_hbm.at[pl.ds(j * rows, rows)], k.at[j], sem.at[j]) for j in range(parts)]
    start_all(copies)
    inv, spoil = inverse_parts(g_ref, math.exp(-LIMIT), math.exp(LIMIT))
    blocks, width = len(inv), inv[0].shape[1]
    half = blocks // 2
    lhs = [stack3(v) for v in inv[:half]]
    per = width // rows
    for j in range(parts):
        copies[j].wait()
        acc = jnp.zeros((16, rows), F32)
        for c in range(half):
            acc = acc + lax.dot_general(
                lhs[c], k[j, :, c * width : (c + 1) * width], NT, preferred_element_type=F32
            )
        lanes = jnp.zeros((rows, 128), F32)
        for c in range(half, blocks):
            for g in range(0, width, 128):
                at = c * width + g
                lanes = lanes + k[j, :, at : at + 128].astype(F32) * inv[c][:, g : g + 128]
        start = (j % per) * rows
        at = slice(start, start + rows)
        out = (acc[0:1] + acc[1:2] + acc[2:3] + lane_totals(lanes)) * ratio[j // per, :, at]
        put(o_ref, j // per, at, out + spoil)


def weighted_sums(kernel, gathered, ratio, k, copies, after=()):
    n = k.shape[0]
    blocks, width = BLOCKS, gathered.shape[3]
    parts = n // ROWS
    last = kernel is last_column_kernel
    shape = (parts, ROWS, n) if kernel is row_kernel else (parts, n, ROWS)
    return pl.pallas_call(
        kernel,
        in_specs=[WHOLE, WHOLE, ANYWHERE] + [SCALARS] * last + [ANYWHERE] * (len(after) - last),
        out_specs=WHOLE,
        out_shape=jax.ShapeDtypeStruct((copies, blocks + last, 1, width), F32),
        scratch_shapes=[pltpu.VMEM(shape, BF16), pltpu.SemaphoreType.DMA((parts,))]
        + ([pltpu.VMEM((blocks, 1, width), F32)] if last else []),
        compiler_params=pltpu.CompilerParams(vmem_limit_bytes=44 << 20),
        cost_estimate=LIGHT,
        name="row_sums" if kernel is row_kernel else "column_sums",
    )(gathered, ratio, *far([k]), *after[:last], *far(after[last:]))


def cut_kernel(x_ref, *refs):
    start = 0
    for out in refs[-len(PARTS) :]:
        rows = out.shape[1]
        out[...] = x_ref[:, start : start + rows, :]
        start += rows


def cut(x, after):
    whole = x.shape[1] // sum(PARTS)
    return pl.pallas_call(
        cut_kernel,
        in_specs=[WHOLE] + [ANYWHERE] * len(after),
        out_specs=[WHOLE] * len(PARTS),
        out_shape=[jax.ShapeDtypeStruct((x.shape[0], rows * whole, x.shape[2]), x.dtype) for rows in PARTS],
        compiler_params=pltpu.CompilerParams(vmem_limit_bytes=16 << 20),
        cost_estimate=LIGHT,
        name="cut_rows",
    )(x, *far(after))


def gate_kernel(x_ref, *refs):
    refs[-1][...] = jnp.broadcast_to(x_ref[...], refs[-1].shape)


def gate(x, copies, after):
    return pl.pallas_call(
        gate_kernel,
        in_specs=[WHOLE] + [ANYWHERE] * len(after),
        out_specs=WHOLE,
        out_shape=jax.ShapeDtypeStruct((copies,) + x.shape[1:], x.dtype),
        cost_estimate=LIGHT,
        name="gate",
    )(x, *after)


def potentials_kernel(homes, row_ref, col_ref, row_pot, column_pot, tile_row):
    rows = jnp.sum(row_ref[:, :BLOCKS], axis=0)
    columns = jnp.sum(col_ref[:, :BLOCKS], axis=0)
    for b in range(BLOCKS):
        row_pot[b : b + 1] = -jnp.log(rows[b])
        column_pot[b : b + 1] = -jnp.log(columns[b])
    for j in range(tile_row.shape[0]):
        tile_row[j : j + 1] = col_ref[homes[j], BLOCKS]


def potentials(row_gathered, gathered, homes):
    width = gathered.shape[3]
    return pl.pallas_call(
        potentials_kernel,
        in_specs=[SCALARS, WHOLE, WHOLE],
        out_specs=[WHOLE] * 3,
        out_shape=[jax.ShapeDtypeStruct((n, width), F32) for n in (BLOCKS, BLOCKS, homes.shape[0])],
        cost_estimate=LIGHT,
        name="potentials",
    )(homes, row_gathered, gathered)


def pick_kernel(ids, table, first, *refs):
    del first
    outs, buf, come, go = refs[:-3], refs[-3], refs[-2], refs[-1]
    groups, tiles = buf.shape[:2]

    def fetch(i, j):
        return pltpu.make_async_copy(table.at[ids[i, j]], buf.at[i, j], come.at[i, j])

    for i in range(groups):
        start_all([fetch(i, j) for j in range(tiles)])
    stores = [pltpu.make_async_copy(buf.at[i], outs[i], go.at[i]) for i in range(groups)]
    for i in range(groups):
        wait_all([fetch(i, j) for j in range(tiles)])
        stores[i].start()
    wait_all(stores)


def pick(table, ids, after):
    groups, tiles = ids.shape
    shape = (tiles,) + table.shape[1:]
    return pl.pallas_call(
        pick_kernel,
        in_specs=[SCALARS, ANYWHERE, ANYWHERE],
        out_specs=[ANYWHERE] * groups,
        out_shape=[jax.ShapeDtypeStruct(shape, table.dtype)] * groups,
        scratch_shapes=[
            pltpu.VMEM((groups,) + shape, table.dtype),
            pltpu.SemaphoreType.DMA((groups, tiles)),
            pltpu.SemaphoreType.DMA((groups,)),
        ],
        compiler_params=pltpu.CompilerParams(vmem_limit_bytes=16 << 20),
        cost_estimate=LIGHT,
        name="pick_pieces",
    )(ids, *far([table]), after)


def posterior_kernel(scale, count, tile_tgt, places, *refs):
    x_hbm, refs = refs[:count], refs[count:]
    y_hbm, r_ref, c_ref, o_hbm, x, y, o, x_sem, y_sem, o_sem = refs
    tiles, width, depth = x.shape
    groups = count // len(PARTS)
    piece = width // groups
    cuts = o_sem.shape[1]
    rows = width // cuts

    def x_copies(j):
        copies = []
        for part in range(len(PARTS)):
            for p in range(groups):
                src = x_hbm[part * groups + p]
                at = places[p] * piece + sum(x_hbm[earlier * groups].shape[1] for earlier in range(part))
                rows = pl.ds(pl.multiple_of(at, 16), src.shape[1])
                copies.append(pltpu.make_async_copy(src.at[j], x.at[j, rows], x_sem.at[j, part, p]))
        return copies

    def y_copy(j):
        return pltpu.make_async_copy(y_hbm.at[tile_tgt[j]], y.at[j], y_sem.at[j])

    def o_copy(j, q):
        at = pl.ds(q * rows, rows)
        return pltpu.make_async_copy(o.at[j, at], o_hbm.at[0, 0, j, at], o_sem.at[j, q])

    def fetch(j):
        y_copy(j).start()
        start_all(x_copies(j))

    fetch(0)
    fetch(1)

    def step(j, carry):
        @pl.when(j + 2 < tiles)
        def _():
            fetch(j + 2)

        y_copy(j).wait()
        wait_all(x_copies(j))
        col = c_ref[pl.ds(tile_tgt[j], 1), :]
        for q in range(cuts):
            at = slice(q * rows, (q + 1) * rows)
            row = jnp.broadcast_to(r_ref[pl.ds(j, 1), at], (128, rows)).T
            for start in range(0, width, 256):
                s = lax.dot_general(x[j, at], y[j, start : start + 256], NT, preferred_element_type=F32) * scale
                for g in range(0, 256, 128):
                    cols = slice(start + g, start + g + 128)
                    o[j, at, cols] = s[:, g : g + 128] + row + col[:, cols]
            o_copy(j, q).start()
        return carry

    lax.fori_loop(0, tiles, step, 0)
    for j in range(tiles):
        wait_all([o_copy(j, q) for q in range(cuts)])


def posterior(pieces, places, targets, tile_row, column_pot, tile_tgt):
    tiles, _, depth = pieces[0].shape
    width = targets.shape[1]
    cuts = 2
    return pl.pallas_call(
        functools.partial(posterior_kernel, 2.0 / math.sqrt(depth), len(pieces)),
        in_specs=[SCALARS, SCALARS] + [ANYWHERE] * (len(pieces) + 1) + [WHOLE, WHOLE],
        out_specs=ANYWHERE,
        scratch_shapes=[
            pltpu.VMEM((tiles, width, depth), BF16),
            pltpu.VMEM((tiles, width, depth), BF16),
            pltpu.VMEM((tiles, width, width), F32),
            pltpu.SemaphoreType.DMA((tiles, len(PARTS), len(pieces) // len(PARTS))),
            pltpu.SemaphoreType.DMA((tiles,)),
            pltpu.SemaphoreType.DMA((tiles, cuts)),
        ],
        out_shape=jax.ShapeDtypeStruct((1, 1, tiles, width, width), F32),
        compiler_params=pltpu.CompilerParams(vmem_limit_bytes=54 << 20),
        cost_estimate=LIGHT,
        name="posterior",
    )(tile_tgt, places, *far([*pieces, targets]), tile_row, column_pot)


def swap(x, axis):
    return lax.all_to_all(x, axis, split_axis=0, concat_axis=0, tiled=True)


def torus_pieces(parts, side):
    def shift(x, axis, by):
        def to(i):
            a, b = divmod(i, side)
            a, b = ((a + by) % side, b) if axis == 0 else (a, (b + by) % side)
            return a * side + b

        return lax.ppermute(x, "src", [(i, to(i)) for i in range(side * side)])

    pieces = []
    lines = []
    for route, part in enumerate(parts):
        lines.append(jnp.stack([part] + [shift(part, route, k) for k in range(1, side)]))
    back = [shift(line, 1 - route, 1) for route, line in enumerate(lines)]
    ahead = [shift(line, 1 - route, -1) for route, line in enumerate(lines)]
    mid = side // 2
    for route, line in enumerate(lines):
        far = [shift(back[route][:mid], 1 - route, 1), shift(ahead[route][mid:], 1 - route, -1)]
        pieces += [line, back[route], *far, ahead[route]]
    return pieces


def on_device(source_emb, target_emb, slot_source, slot_target):
    src_blocks, tgt_blocks = source_emb.shape[0], target_emb.shape[0]
    src_count, tgt_count = lax.axis_size("src"), lax.axis_size("tgt")
    own_row, own_col = lax.axis_index("src"), lax.axis_index("tgt")
    tiles = slot_source.shape[2]
    tile_src = slot_source[0, 0]
    tile_tgt = slot_target[0, 0] - own_col * tgt_blocks
    tile_home = tile_src // src_blocks

    cores = 2
    length = tgt_count // cores
    turns = [(far, other) for far in range(length) for other in range(cores)]

    def turned(t, far, other):
        return (t // cores + far) % length * cores + (t % cores + other) % cores

    def turn(x, far, other):
        return lax.ppermute(x, "tgt", [(t, turned(t, far, other)) for t in range(tgt_count)])

    places = jnp.stack([turned(own_col, length - far, other) for far, other in turns])

    whole_blocks = lax.all_gather(source_emb, "tgt", axis=1, tiled=True)
    side = math.isqrt(src_count)
    target_pieces = torus_pieces((target_emb[: tgt_blocks // 2], target_emb[tgt_blocks // 2 :]), side)

    slots = jnp.concatenate([slot_source[0, 0], slot_target[0, 0]])
    slots = jnp.pad(slots, (0, 128 - 2 * tiles))[None, None]
    column_slots = swap(jnp.broadcast_to(slots, (src_count, 1, 128)), "src")[:, 0]
    named_src = column_slots[:, :tiles].reshape(-1) - own_row * src_blocks
    named_tgt = column_slots[:, tiles : 2 * tiles].reshape(-1) - own_col * tgt_blocks
    named = jnp.any(
        (named_src[:, None, None] == jnp.arange(src_blocks)[None, :, None])
        & (named_tgt[:, None, None] == jnp.arange(tgt_blocks)[None, None, :]),
        axis=0,
    ).astype(jnp.int32)
    plan_column = home_plan(column_slots[:, :tiles], own_row, src_blocks)

    aimed = jnp.stack([turned(own_col, far, other) for far, other in turns])
    slot_row = jnp.pad(tile_src.astype(F32), (0, target_emb.shape[1] * src_count - tiles))[None]
    shards = cut(source_emb, [whole_blocks, named] + target_pieces)
    tables = [lax.all_gather(shard, "src", axis=0, tiled=True) for shard in shards]
    where = jnp.stack([own_row // side, own_row % side])
    weights, sums, ratio, targets = score_weights(whole_blocks, target_pieces, where, named, slot_row, tgt_count, side, shards)
    pieces = [[None] * len(turns) for _ in PARTS]
    windows = [[(0, [0, 2, 6, 3, 7, 4])], [(0, [1, 5]), (1, [0, 2, 6, 4])], [(1, [1, 3, 7, 5])]]
    for iteration, window in enumerate(windows):
        if iteration:
            sums = weighted_sums(row_kernel, gathered, ratio, weights, 1, after=picked)
            sums = gate(sums, tgt_count, arrived)
        row_gathered = swap(sums, "tgt")
        if not iteration:
            aims = row_gathered[:, BLOCKS, 0, :tiles].astype(jnp.int32)[aimed]
        picked, arrived = [], []
        for number, (part, chosen) in enumerate(window):
            if number:
                sums = weighted_sums(column_kernel, row_gathered, ratio, weights, src_count, after=picked)
            taken = pick(tables[part], aims[jnp.array(chosen)], sums if number else row_gathered)
            for x, i in zip(taken, chosen):
                pieces[part][i] = turn(x, *turns[i]) if i else x
                picked.append(x)
                arrived.append(pieces[part][i])
        if iteration == ITERS - 1:
            sums = weighted_sums(last_column_kernel, row_gathered, ratio, weights, src_count, after=[plan_column, *picked])
        elif len(window) == 1:
            sums = weighted_sums(column_kernel, row_gathered, ratio, weights, src_count, after=picked)
        gathered = swap(sums, "src")
    pieces = pieces[0] + pieces[1]

    row_pot, column_pot, tile_row = potentials(row_gathered, gathered, tile_home)

    def unfinished(carry):
        return carry[0]

    def redo(carry):
        zeros = [jnp.zeros_like(carry[1]), jnp.zeros_like(carry[3])]
        scores = posterior(pieces, places, targets, zeros[1], zeros[0], tile_tgt)[0, 0]
        potentials = log_domain(scores, tile_home, tile_tgt, plan_column, src_blocks, tgt_blocks)
        return (jnp.zeros((), jnp.bool_),) + potentials

    out_of_range = jnp.isnan(jnp.sum(row_gathered[:, 0, 0, 0]))
    carry = (out_of_range, column_pot, row_pot, tile_row)
    _, column_pot, row_pot, tile_row = lax.while_loop(unfinished, redo, carry)
    log_post = posterior(pieces, places, targets, tile_row, column_pot, tile_tgt)
    return (log_post, row_pot, column_pot)


def solution(mesh):
    placed = (
        P("src", "tgt", None),
        P("tgt", "src", None),
        P("src", "tgt", None),
        P("src", "tgt", None),
    )
    return jax.shard_map(
        on_device,
        mesh=mesh,
        in_specs=placed,
        out_specs=(P("src", "tgt", None, None, None), P("src", None), P("tgt", None)),
        check_vma=False,
    )
```
